32 devices in a mesh: gx: 4 (over x, core), gy: 2 (over y), gz: 4 (over z).
Axes of the slice: x: 2, y: 2, z: 4, core: 2. Of those that a mesh axis runs over, the one named last changes fastest.
Arguments:
- features: float32 [128, 64, 512], P(('gx', 'gy', 'gz')), may hold values from -6 to 6
- preact: float32 [128, 64, 512], P(('gx', 'gy', 'gz')), may hold values from -10 to 10
- cotangent: float32 [128, 64, 512], P(('gx', 'gy', 'gz')), may hold values from -6 to 6
- kernel: float32 [27, 64, 64], replicated, may hold values from -0.15625 to 0.15625
- active: int32 [128, 512], P(('gx', 'gy', 'gz')), may hold values from 0 to 1, as said below
- owner_dir: int32 [128, 27], P(('gx', 'gy', 'gz')), may hold values from 0 to 27, as said below
- owner_slot: int32 [128, 27], P(('gx', 'gy', 'gz')), may hold values from 0 to 3, as said below
- send_list: int32 [96], P(('gx', 'gy', 'gz')), may hold values from 0 to 4, as said below
Outputs:
- input_grad: float32 [128, 64, 512], P(('gx', 'gy', 'gz'))
- kernel_grad: float32 [27, 64, 64], replicated
- bias_grad: float32 [64], replicated
The draws below stay inside these ranges and needn't reach their ends.
Inputs may be any that keep to these rules, and one draw needn't show every extreme that they name: `owner_dir`: 27 where the neighbouring block is empty or the stored entry is unused; 13 for a block of the same partition; else the offset of the owner's grid position, 9 (dx + 1) + 3 (dy + 1) + (dz + 1), with dx, dy, dz each -1, 0 or 1. A named partition always exists and lists the block in its send list. `owner_slot`: own stored index where owner_dir is 13, position in the owner's send list where owner_dir names another partition, 0 where it is 27. `send_list`: each partition's 3 entries hold, increasing, the distinct stored indices of its occupied blocks in the partition's outer layer of blocks (on faces, edges or corners), each of which touches another partition, then 4 for unused entries; some partition fills all 3. 1 for active voxels of an occupied stored block, 0 elsewhere; unused stored entries are 0 throughout; some partition has all 4 entries occupied.
All inputs are finite; a program needn't handle non-finite values.
Results may differ from the reference program's by a relative error of at most 0.0001.
Values sent between devices are 32-bit elements; how exact they have to be, the bound alone decides.
A program may use at most 64 MiB of HBM per device.

```python
import jax
import jax.numpy as jnp
from jax import lax

C = 64
BS = 8
PB = 6
SEND = 3
BLK_DEV = 4
VOL = 512
NB_ALL = 128
N_GX = 4
N_GY = 2
N_GZ = 4


def block_layout(key):
    subkeys = jax.random.split(jax.random.fold_in(key, 7), 12)
    size_x, size_y, size_z = (N_GX, N_GY, N_GZ)
    devices = size_x * size_y * size_z
    part_side = PB
    slot_count = part_side ** 3
    inner_side = part_side - 2
    device_ids = jnp.arange(devices, dtype=jnp.int32)
    coord_x = device_ids // (size_y * size_z)
    coord_y = device_ids // size_z % size_y
    coord_z = device_ids % size_z
    slot_ids = jnp.arange(slot_count, dtype=jnp.int32)
    local_x = slot_ids // (part_side * part_side)
    local_y = slot_ids // part_side % part_side
    local_z = slot_ids % part_side
    forced_x = jax.random.randint(subkeys[0], (), 0, size_x - 1)
    forced_y = jax.random.randint(subkeys[1], (), 0, size_y - 1)
    forced_z = jax.random.randint(subkeys[2], (), 0, size_z - 1)
    parity_flag = (forced_x + forced_y + forced_z) % 2
    creator = (coord_x + coord_y + coord_z) % 2 == parity_flag
    forced = (forced_x * size_y + forced_y) * size_z + forced_z
    is_forced = device_ids == forced
    link_draw = jax.random.randint(subkeys[3], (devices, 3), 0, 10) < 6
    has_next = jnp.stack([coord_x < size_x - 1, coord_y < size_y - 1, coord_z < size_z - 1], axis=1)
    link_on = creator[:, None] & has_next & (link_draw | is_forced[:, None])
    spot_first = jax.random.randint(subkeys[4], (devices, 3), 0, part_side)
    spot_second = jax.random.randint(subkeys[5], (devices, 3), 0, part_side)
    inner_first = jax.random.randint(subkeys[6], (devices, 3), 1, part_side - 1)
    inner_second = jax.random.randint(subkeys[7], (devices, 3), 1, part_side - 1)
    spot_first = jnp.where(is_forced[:, None], inner_first, spot_first)
    spot_second = jnp.where(is_forced[:, None], inner_second, spot_second)
    rim_count = jnp.zeros((devices, slot_count), jnp.int32)
    strides = [size_y * size_z, size_z, 1]
    for axis_index in range(3):
        first = spot_first[:, axis_index]
        second = spot_second[:, axis_index]
        link_value = link_on[:, axis_index].astype(jnp.int32)
        if axis_index == 0:
            source_slot = ((part_side - 1) * part_side + first) * part_side + second
            target_slot = first * part_side + second
        elif axis_index == 1:
            source_slot = (first * part_side + part_side - 1) * part_side + second
            target_slot = first * part_side * part_side + second
        else:
            source_slot = (first * part_side + second) * part_side + part_side - 1
            target_slot = (first * part_side + second) * part_side
        target_dev = jnp.where(link_value > 0, device_ids + strides[axis_index], device_ids)
        rim_count = rim_count.at[device_ids, source_slot].max(link_value)
        rim_count = rim_count.at[target_dev, target_slot].max(link_value)
    rim_live = rim_count > 0
    inner_slot = (local_x >= 1) & (local_x <= part_side - 2) & (local_y >= 1) & (local_y <= part_side - 2) & (local_z >= 1) & (local_z <= part_side - 2)
    rim_slot = jnp.logical_not(inner_slot)
    inner_index = jnp.where(inner_slot, ((local_x - 1) * inner_side + (local_y - 1)) * inner_side + (local_z - 1), 0)
    capacity = BLK_DEV - SEND
    heavy_part = jax.random.randint(subkeys[8], (devices,), 0, 4) == 0
    light_count = jax.random.randint(subkeys[9], (devices,), 0, 2)
    counts = jnp.where(heavy_part | is_forced, capacity, light_count)
    inner_total = inner_side ** 3
    scores = jax.random.randint(subkeys[10], (devices, inner_total), 0, 2 ** 20) * inner_total + jnp.arange(inner_total, dtype=jnp.int32)[None, :]
    ranking = jnp.argsort(jnp.argsort(scores, axis=1), axis=1).astype(jnp.int32)
    inner_live = inner_slot[None, :] & (ranking[:, inner_index] < counts[:, None])
    occupied = rim_live | inner_live
    priority = jax.random.randint(subkeys[11], (devices, slot_count), 0, 2 ** 20) * slot_count + slot_ids[None, :]
    priority = jnp.where(occupied, priority, priority + 2 ** 30)
    stored_slot = jnp.argsort(priority, axis=1)[:, :BLK_DEV].astype(jnp.int32)
    stored_live = jnp.take_along_axis(occupied, stored_slot, axis=1)
    store_ids = jnp.arange(BLK_DEV, dtype=jnp.int32)
    slot_store = jnp.zeros((devices, slot_count), jnp.int32).at[device_ids[:, None], stored_slot].set(jnp.broadcast_to(store_ids[None, :], (devices, BLK_DEV)))
    stored_rim = rim_slot[stored_slot] & stored_live
    position = jnp.cumsum(stored_rim.astype(jnp.int32), axis=1) - 1
    send_rows = []
    for position_index in range(SEND):
        matched = stored_rim & (position == position_index)
        found_index = jnp.sum(jnp.where(matched, store_ids[None, :], 0), axis=1) + jnp.where(jnp.any(matched, axis=1), 0, BLK_DEV)
        send_rows.append(found_index)
    send_table = jnp.stack(send_rows, axis=1).astype(jnp.int32)
    store_position = jnp.where(stored_rim, position, 0)
    offsets = jnp.arange(27, dtype=jnp.int32)
    shift_x = offsets // 9 - 1
    shift_y = offsets // 3 % 3 - 1
    shift_z = offsets % 3 - 1
    global_x = coord_x[:, None, None] * part_side + local_x[stored_slot][:, :, None] + shift_x[None, None, :]
    global_y = coord_y[:, None, None] * part_side + local_y[stored_slot][:, :, None] + shift_y[None, None, :]
    global_z = coord_z[:, None, None] * part_side + local_z[stored_slot][:, :, None] + shift_z[None, None, :]
    inside = (global_x >= 0) & (global_x < size_x * part_side) & (global_y >= 0) & (global_y < size_y * part_side) & (global_z >= 0) & (global_z < size_z * part_side)
    global_x = jnp.clip(global_x, 0, size_x * part_side - 1)
    global_y = jnp.clip(global_y, 0, size_y * part_side - 1)
    global_z = jnp.clip(global_z, 0, size_z * part_side - 1)
    owner_x = global_x // part_side
    owner_y = global_y // part_side
    owner_z = global_z // part_side
    owner_dev = (owner_x * size_y + owner_y) * size_z + owner_z
    near_slot = (global_x % part_side * part_side + global_y % part_side) * part_side + global_z % part_side
    near_live = occupied[owner_dev, near_slot] & inside & stored_live[:, :, None]
    direction = (owner_x - coord_x[:, None, None] + 1) * 9 + (owner_y - coord_y[:, None, None] + 1) * 3 + (owner_z - coord_z[:, None, None] + 1)
    own_store = slot_store[owner_dev, near_slot]
    remote = store_position[owner_dev, own_store]
    dir_table = jnp.where(near_live, direction, 27).astype(jnp.int32)
    slot_table = jnp.where(near_live, jnp.where(direction == 13, own_store, remote), 0).astype(jnp.int32)
    return (stored_live, dir_table.reshape(devices * BLK_DEV, 27), slot_table.reshape(devices * BLK_DEV, 27), send_table.reshape(devices * SEND))


def draw_active(key, part):
    stored_live = block_layout(key)[0]
    devices = N_GX * N_GY * N_GZ
    flips = jax.random.randint(jax.random.fold_in(key, 11), (devices * BLK_DEV, BS ** 3), 0, 10) < 6
    return (flips & stored_live.reshape(devices * BLK_DEV)[:, None]).astype(jnp.int32)


def draw_owner_dir(key, part):
    return block_layout(key)[1]


def draw_owner_slot(key, part):
    return block_layout(key)[2]


def draw_send_list(key, part):
    return block_layout(key)[3]


def block_scale(key, shape, shards, smallest, top_value):
    def one(axis_at, parts):
        heights = jax.random.uniform(jax.random.fold_in(jax.random.fold_in(key, 6), axis_at), (parts,), jnp.float32, smallest / len(shards), top_value / len(shards))
        return jnp.repeat(jnp.exp(heights), shape[axis_at] // parts).reshape((-1,) + (1,) * (len(shape) - axis_at - 1))

    loudness = one(*shards[0])
    for cut in shards[1:]:
        loudness = loudness * one(*cut)
    return loudness


def noise(key, dims, spread, bound, cuts=(), kind=jnp.bfloat16):
    drawn = jax.random.normal(key, dims, jnp.float32) * spread
    if len(cuts) > 0:
        drawn = block_scale(key, dims, cuts, -0.22, 0.18) * drawn
    return jnp.clip(drawn, min=-bound, max=bound).astype(kind)


def setup_inputs(seed: int = 0) -> dict:
    streams_of = jax.random.split(jax.random.key(seed), 9)
    features = noise(streams_of[0], (NB_ALL, C, VOL), 1.0, 6.0, ((0, 32),), jnp.float32)
    preact = noise(streams_of[1], (NB_ALL, C, VOL), 2.0, 10.0, ((0, 32),), jnp.float32)
    cotangent = noise(streams_of[2], (NB_ALL, C, VOL), 1.0, 6.0, ((0, 32),), jnp.float32)
    kernel = noise(streams_of[3], (27, C, C), (27 * C) ** -0.5, 0.15625, (), jnp.float32)
    active = draw_active(jax.random.fold_in(streams_of[8], 71), 0)
    owner_dir = draw_owner_dir(jax.random.fold_in(streams_of[8], 71), 0)
    owner_slot = draw_owner_slot(jax.random.fold_in(streams_of[8], 71), 0)
    send_list = draw_send_list(jax.random.fold_in(streams_of[8], 71), 0)
    return dict(features=features, preact=preact, cotangent=cotangent, kernel=kernel, active=active, owner_dir=owner_dir, owner_slot=owner_slot, send_list=send_list)


def silu_slope(preact):
    sigmoid_value = jax.nn.sigmoid(preact)
    return sigmoid_value * (1.0 + preact * (1.0 - sigmoid_value))


def neighbourhood(source, targets, extent):
    anchor = jnp.zeros((), jnp.int32)
    channels = source.shape[1]
    layers = []
    for place_x in range(3):
        strips = []
        for place_y in range(3):
            pieces = []
            for place_z in range(3):
                places = (place_x, place_y, place_z)
                begins = [anchor + (extent - 1 if where_at == 0 else 0) for where_at in places]
                lengths = [extent if where_at == 1 else 1 for where_at in places]
                chosen = targets[place_x * 9 + place_y * 3 + place_z].astype(jnp.int32)
                portion = lax.dynamic_slice(source, [chosen, anchor] + begins, [1, channels] + lengths)
                pieces.append(portion[0])
            strips.append(jnp.concatenate(pieces, axis=3))
        layers.append(jnp.concatenate(strips, axis=2))
    return jnp.concatenate(layers, axis=1)


def shifted_stack(padded, direction, extent):
    windows = []
    for offset_x in (-1, 0, 1):
        for offset_y in (-1, 0, 1):
            for offset_z in (-1, 0, 1):
                begin_x = 1 + direction * offset_x
                begin_y = 1 + direction * offset_y
                begin_z = 1 + direction * offset_z
                window = padded[:, begin_x:begin_x + extent, begin_y:begin_y + extent, begin_z:begin_z + extent]
                windows.append(window.reshape(padded.shape[0], extent ** 3))
    return jnp.stack(windows)


def reference(features, preact, cotangent, kernel, active, owner_dir, owner_slot, send_list):
    blocks_all, channels, volume = features.shape
    extent = BS
    devices = N_GX * N_GY * N_GZ
    block_ids = jnp.arange(blocks_all, dtype=jnp.int32)
    device_ids = block_ids // BLK_DEV
    coord_x = device_ids // (N_GY * N_GZ)
    coord_y = (device_ids // N_GZ) % N_GY
    coord_z = device_ids % N_GZ
    step_x = owner_dir // 9 - 1
    step_y = (owner_dir // 3) % 3 - 1
    step_z = owner_dir % 3 - 1
    owner_dev = ((coord_x[:, None] + step_x) * N_GY + coord_y[:, None] + step_y) * N_GZ + coord_z[:, None] + step_z
    owner_dev = jnp.clip(owner_dev, 0, devices - 1).astype(jnp.int32)
    listed = send_list[jnp.clip(owner_dev * SEND + owner_slot, 0, devices * SEND - 1)]
    remote_index = owner_dev * BLK_DEV + jnp.clip(listed, 0, BLK_DEV - 1)
    local_index = device_ids[:, None] * BLK_DEV + owner_slot
    source_index = jnp.where(owner_dir == 13, local_index, remote_index)
    source_index = jnp.where(owner_dir < 27, source_index, 0).astype(jnp.int32)
    valid_mask = (owner_dir < 27).astype(jnp.float32)
    every_place = jnp.arange(27, dtype=jnp.int32)

    def visit_block(running, inputs):
        kernel_partial, bias_partial = running
        indices, weights, block_index = inputs
        near_mask = active[indices].astype(jnp.float32)[:, None, :] * weights[:, None, None]
        near_grad = cotangent[indices] * silu_slope(preact[indices]) * near_mask
        near_input = features[indices] * near_mask
        cube_shape = (27, channels, extent, extent, extent)
        grad_windows = shifted_stack(neighbourhood(near_grad.reshape(cube_shape), every_place, extent), -1, extent)
        input_windows = shifted_stack(neighbourhood(near_input.reshape(cube_shape), every_place, extent), 1, extent)
        block_mask = active[block_index].astype(jnp.float32)[None, :]
        own_grad = cotangent[block_index] * silu_slope(preact[block_index]) * block_mask
        block_result = jnp.einsum("kio,kov->iv", kernel, grad_windows, precision=lax.Precision.HIGHEST) * block_mask
        kernel_partial = kernel_partial + jnp.einsum("kiv,ov->kio", input_windows, own_grad, precision=lax.Precision.HIGHEST)
        bias_partial = bias_partial + jnp.sum(own_grad, axis=1)
        return (kernel_partial, bias_partial), block_result

    initial = (jnp.zeros((27, channels, channels), jnp.float32), jnp.zeros((channels,), jnp.float32))
    (kernel_partial, bias_partial), input_grad = lax.scan(visit_block, initial, (source_index, valid_mask, block_ids))
    scaling = (volume * blocks_all) ** -0.5
    return input_grad, kernel_partial * scaling, bias_partial * scaling
```

```python
import functools
import itertools

import jax
import jax.numpy as jnp
from jax import lax
from jax.experimental import pallas as pl
from jax.experimental.pallas import tpu as pltpu
from jax.sharding import PartitionSpec as P

BS = 8
LANES = 128
AXES = ("gx", "gy", "gz")
MESH = pl.DeviceIdType.MESH
DEPTH = 3 * BS
CUBE_STEPS = ((BS + 2) * DEPTH, DEPTH, 1)
BLOCK_STEPS = (BS * BS, BS, 1)
HEADINGS = [m for m in itertools.product((-1, 0, 1), repeat=3) if m != (0, 0, 0)]
FACES = [m for m in HEADINGS if sum(map(abs, m)) == 1]
EDGES = [m for m in HEADINGS if sum(map(abs, m)) == 2]
CORNERS = [m for m in HEADINGS if sum(map(abs, m)) == 3]
GROUPS = (FACES, EDGES, CORNERS)


def silu_slope(preact):
    sigmoid_value = jax.nn.sigmoid(preact)
    return sigmoid_value * (1.0 + preact * (1.0 - sigmoid_value))


def place(move):
    group = sum(map(abs, move)) - 1
    return group, GROUPS[group].index(move)


def side_row(move):
    return sum(step * (BS - 1) for step, m in zip(BLOCK_STEPS, move) if m == 1)


def free_axes(move):
    return [axis for axis in range(3) if move[axis] == 0]


def split_lanes(value):
    high = value.astype(jnp.bfloat16).astype(jnp.float32)
    return high + pltpu.roll(value - high, LANES // 2, 1)


def halo_kernel(
    sizes, send_list, preact, cotangent, active, weights, split_grad, split_weights, bias,
    face_in, edge_in, corner_in, grad, picked, face_out, edge_out, corner_out, send_sem, recv_sem,
):
    blocks, channels, volume = preact.shape
    listed = send_list.shape[0]
    here = [lax.axis_index(axis) for axis in AXES]

    def inside(move):
        checks = []
        for axis in range(3):
            if move[axis] == 1:
                checks.append((here[axis] < sizes[axis] - 1).astype(jnp.int32))
            elif move[axis] == -1:
                checks.append((here[axis] > 0).astype(jnp.int32))
        return functools.reduce(lambda a, b: a * b, checks)

    live = {move: inside(move) for move in HEADINGS}
    target = {move: tuple(h + m for h, m in zip(here, move)) for move in HEADINGS}
    barrier = pltpu.get_barrier_semaphore()
    for move in HEADINGS:
        @pl.when(live[move] == 1)
        def _():
            pl.semaphore_signal(barrier, inc=1, device_id=target[move], device_id_type=MESH)

    total = jnp.zeros((1, LANES), jnp.float32)
    for b in range(blocks):
        value = cotangent[b] * silu_slope(preact[b]) * active[pl.ds(b, 1), :].astype(jnp.float32)
        rows = jnp.concatenate([value, jnp.zeros((LANES - channels, volume), jnp.float32)], axis=0).T
        grad[b] = rows
        total = total + jnp.sum(rows, axis=0, keepdims=True)
    bias[...] = jnp.broadcast_to(total, bias.shape)

    for s in range(listed):
        entry = send_list[s]
        keep = (entry < blocks).astype(jnp.float32)
        picked[...] = grad[jnp.minimum(entry, blocks - 1)] * keep
        for f, move in enumerate(FACES):
            first, second = free_axes(move)
            base = side_row(move)
            tiles = [
                picked[pl.ds(base + u * BLOCK_STEPS[first], BS, stride=BLOCK_STEPS[second]), :]
                for u in range(BS)
            ]
            for u in range(BS // 2):
                face_out[f, s, pl.ds(u * BS, BS), :] = tiles[u] + pltpu.roll(
                    tiles[u + BS // 2], LANES // 2, 1
                )
        for f, move in enumerate(EDGES):
            (along,) = free_axes(move)
            edge_out[f, s] = picked[pl.ds(side_row(move), BS, stride=BLOCK_STEPS[along]), :]
        for f, move in enumerate(CORNERS):
            corner_out[f, s] = jnp.broadcast_to(picked[pl.ds(side_row(move), 1), :], (BS, LANES))

    count = functools.reduce(lambda a, b: a + b, [live[move] for move in HEADINGS])
    pl.semaphore_wait(barrier, count)

    sent, landed = (face_out, edge_out, corner_out), (face_in, edge_in, corner_in)

    def copy_of(move):
        group, f = place(move)
        n = HEADINGS.index(move)
        return pltpu.make_async_remote_copy(
            src_ref=sent[group].at[f],
            dst_ref=landed[group].at[f],
            send_sem=send_sem.at[n],
            recv_sem=recv_sem.at[n],
            device_id=target[move],
            device_id_type=MESH,
        )

    for move in FACES + EDGES + CORNERS:
        @pl.when(live[move] == 1)
        def _():
            copy_of(move).start()

    for b in range(blocks):
        split_grad[b] = split_lanes(grad[b])
    for k in range(weights.shape[0]):
        value = weights[k]
        high = value.astype(jnp.bfloat16)
        rest = (value - high.astype(jnp.float32)).astype(jnp.bfloat16)
        column = jnp.concatenate([high, rest], axis=0)
        split_weights[:, pl.ds(k * LANES, LANES)] = jnp.concatenate([column, column], axis=1)

    for move in FACES + EDGES + CORNERS:
        back = tuple(-m for m in move)

        @pl.when(live[move] == 1)
        def _():
            copy_of(move).wait_send()

        @pl.when(live[back] == 1)
        def _():
            copy_of(move).wait_recv()


def conv_kernel(
    owner_dir, owner_slot, split_grad, face_in, edge_in, corner_in, features, active,
    split_weights, input_grad, partial, cube, windows, wide,
):
    blocks, channels, volume = features.shape
    taps = split_weights.shape[1] // LANES
    low_half = lax.broadcasted_iota(jnp.int32, (BS, LANES), 1) < LANES // 2
    wide[...] = jnp.zeros_like(wide)

    def cube_row(move):
        origin = CUBE_STEPS[0] + CUBE_STEPS[1] + BS
        return origin + sum(
            step * (BS if m == 1 else -1) for step, m in zip(CUBE_STEPS, move) if m != 0
        )

    def fill_own(offset, slot):
        back = tuple(-m for m in offset)
        source, into = side_row(back), cube_row(offset)
        free = free_axes(offset)
        if not free:
            cube[pl.ds(into, 1), :] = split_grad[slot, pl.ds(source, 1), :]
            return
        along = free[-1]
        for lead in itertools.product(range(BS), repeat=len(free) - 1):
            shift = sum(BLOCK_STEPS[a] * u for a, u in zip(free, lead))
            move = sum(CUBE_STEPS[a] * u for a, u in zip(free, lead))
            cube[pl.ds(into + move, BS, stride=CUBE_STEPS[along]), :] = split_grad[
                slot, pl.ds(source + shift, BS, stride=BLOCK_STEPS[along]), :
            ]

    def fill_remote(offset, owner, slot):
        group, f = place(tuple(-m for m in owner))
        into = cube_row(offset)
        picks = [BS - 1 if offset[a] == -1 else 0 for a in range(3)]
        if group == 2:
            value = jnp.where(low_half, corner_in[f, slot], 0.0)
            cube[pl.ds(into, 1), :] = split_lanes(value)[:1]
        elif group == 1:
            (along,) = free_axes(owner)
            value = split_lanes(jnp.where(low_half, edge_in[f, slot], 0.0))
            if offset[along] == 0:
                cube[pl.ds(into, BS, stride=CUBE_STEPS[along]), :] = value
            else:
                at = picks[along]
                cube[pl.ds(into, 1), :] = value[at : at + 1]
        else:
            first, second = free_axes(owner)
            for u in range(BS) if offset[first] == 0 else (picks[first],):
                half, row = divmod(u, BS // 2)
                value = face_in[f, slot, pl.ds(row * BS, BS), :]
                if half:
                    value = pltpu.roll(value, LANES // 2, 1)
                value = split_lanes(jnp.where(low_half, value, 0.0))
                at_u = into + (u * CUBE_STEPS[first] if offset[first] == 0 else 0)
                if offset[second] == 0:
                    cube[pl.ds(at_u, BS, stride=CUBE_STEPS[second]), :] = value
                else:
                    at = picks[second]
                    cube[pl.ds(at_u, 1), :] = value[at : at + 1]

    def visit_block(b, carry):
        cube[...] = jnp.zeros_like(cube)
        for x in range(BS):
            for y in range(BS):
                cube[pl.ds(cube_row((0, 0, 0)) + x * CUBE_STEPS[0] + y * CUBE_STEPS[1], BS), :] = (
                    split_grad[b, pl.ds((x * BS + y) * BS, BS), :]
                )
        for offset in HEADINGS:
            o = 9 * (offset[0] + 1) + 3 * (offset[1] + 1) + offset[2] + 1
            code, slot = owner_dir[b, o], owner_slot[b, o]

            @pl.when(code != 27)
            def _():
                @pl.when(code == 13)
                def _():
                    fill_own(offset, slot)

                for owner in itertools.product(*[(0,) if m == 0 else (0, m) for m in offset]):
                    if owner != (0, 0, 0):
                        @pl.when(code == 9 * (owner[0] + 1) + 3 * (owner[1] + 1) + owner[2] + 1)
                        def _():
                            fill_remote(offset, owner, slot)

        for ky in (-1, 0, 1):
            for kz in (-1, 0, 1):
                for x in range(BS + 2):
                    tiles = [
                        cube[pl.ds(x * CUBE_STEPS[0] + (y + 1 - ky) * CUBE_STEPS[1] + BS - kz, BS), :]
                        for y in range(BS)
                    ]
                    windows[3 * (ky + 1) + kz + 1, pl.ds(x * BS * BS, BS * BS), :] = (
                        jnp.concatenate(tiles, axis=0).astype(jnp.bfloat16)
                    )
        whole = jnp.concatenate(
            [
                windows[q, pl.ds((1 - kx) * BS * BS, volume), :]
                for kx in (-1, 0, 1)
                for q in range(9)
            ],
            axis=1,
        )
        mask = active[pl.ds(b, 1), :].astype(jnp.float32)
        result = lax.dot_general(
            whole, split_weights[...], (((1,), (1,)), ((), ())), preferred_element_type=jnp.float32
        )
        result = (result + pltpu.roll(result, LANES // 2, 1)).T
        input_grad[b] = result[:channels] * mask
        masked = features[b] * mask
        high = masked.astype(jnp.bfloat16)
        rest = (masked - high.astype(jnp.float32)).astype(jnp.bfloat16)
        wide[...] += jnp.dot(
            jnp.concatenate([high, rest], axis=0), whole, preferred_element_type=jnp.float32
        )
        return carry

    lax.fori_loop(0, blocks, visit_block, 0)
    half = lax.broadcasted_iota(jnp.int32, (channels, LANES), 1) < LANES // 2

    def summed(k):
        value = wide[:channels, pl.ds(k * LANES, LANES)] + wide[channels:, pl.ds(k * LANES, LANES)]
        return value + pltpu.roll(value, LANES // 2, 1)

    for pair in range((taps + 1) // 2):
        value = summed(2 * pair)
        other = summed(2 * pair + 1) if 2 * pair + 1 < taps else jnp.zeros_like(value)
        partial[pair] = jnp.where(half, value, other)


def shards(sizes, features, preact, cotangent, kernel, active, owner_dir, owner_slot, send_list):
    blocks, channels, volume = features.shape
    listed = send_list.shape[0]
    taps = kernel.shape[0]
    vmem = pl.BlockSpec(memory_space=pltpu.VMEM)
    smem = pl.BlockSpec(memory_space=pltpu.SMEM)
    shaped = jax.ShapeDtypeStruct
    rows = (BS * BS // 2, BS, BS)
    sheets = [(len(g), listed, r, LANES) for g, r in zip(GROUPS, rows)]
    split_grad, split_weights, bias, *landed = pl.pallas_call(
        functools.partial(halo_kernel, sizes),
        out_shape=[
            shaped((blocks, volume, LANES), jnp.float32),
            shaped((2 * channels, taps * LANES), jnp.bfloat16),
            shaped((BS, LANES), jnp.float32),
        ]
        + [shaped(s, jnp.float32) for s in sheets],
        in_specs=[smem, vmem, vmem, vmem, vmem],
        out_specs=[vmem] * 6,
        scratch_shapes=[
            pltpu.VMEM((blocks, volume, LANES), jnp.float32),
            pltpu.VMEM((volume, LANES), jnp.float32),
        ]
        + [pltpu.VMEM(s, jnp.float32) for s in sheets]
        + [pltpu.SemaphoreType.DMA((len(HEADINGS),))] * 2,
        compiler_params=pltpu.CompilerParams(
            collective_id=0, has_side_effects=True, vmem_limit_bytes=40 * 2**20
        ),
        name="halo",
    )(send_list, preact, cotangent, active, kernel)
    input_grad, partial = pl.pallas_call(
        conv_kernel,
        out_shape=[
            shaped((blocks, channels, volume), jnp.float32),
            shaped(((taps + 1) // 2, channels, LANES), jnp.float32),
        ],
        in_specs=[smem, smem] + [vmem] * 7,
        out_specs=[vmem] * 2,
        scratch_shapes=[
            pltpu.VMEM(((BS + 2) * CUBE_STEPS[0], LANES), jnp.float32),
            pltpu.VMEM((9, (BS + 2) * BS * BS, LANES), jnp.bfloat16),
            pltpu.VMEM((2 * channels, taps * LANES), jnp.float32),
        ],
        compiler_params=pltpu.CompilerParams(vmem_limit_bytes=48 * 2**20),
        name="conv",
    )(owner_dir, owner_slot, split_grad, *landed, features, active, split_weights)
    scaling = (volume * blocks * lax.axis_size(AXES)) ** (-0.5)
    total, bias_total = lax.psum((partial, bias), AXES)
    pairs = total.reshape(-1, channels, 2, channels).transpose(0, 2, 1, 3)
    kernel_grad = pairs.reshape(-1, channels, channels)[:taps] * scaling
    return input_grad, kernel_grad, bias_total[0, :channels] * scaling


def solution(mesh):
    whole = P(AXES, None, None)
    table = P(AXES, None)
    sizes = tuple(mesh.shape[axis] for axis in AXES)
    return jax.shard_map(
        functools.partial(shards, sizes),
        mesh=mesh,
        in_specs=(whole, whole, whole, P(), table, table, table, P(AXES)),
        out_specs=(whole, P(), P()),
        check_vma=False,
    )
```

```python
import functools
import itertools

import jax
import jax.numpy as jnp
from jax import lax
from jax.experimental import pallas as pl
from jax.experimental.pallas import tpu as pltpu
from jax.sharding import PartitionSpec as P

BS = 8
LANES = 128
AXES = ("gx", "gy", "gz")
MESH = pl.DeviceIdType.MESH
DEPTH = 3 * BS
CUBE_STEPS = ((BS + 2) * DEPTH, DEPTH, 1)
BLOCK_STEPS = (BS * BS, BS, 1)
HEADINGS = [m for m in itertools.product((-1, 0, 1), repeat=3) if m != (0, 0, 0)]
FACES = [m for m in HEADINGS if sum(map(abs, m)) == 1]
EDGES = [m for m in HEADINGS if sum(map(abs, m)) == 2]
CORNERS = [m for m in HEADINGS if sum(map(abs, m)) == 3]
GROUPS = (FACES, EDGES, CORNERS)


def silu_slope(preact):
    sigmoid_value = jax.nn.sigmoid(preact)
    return sigmoid_value * (1.0 + preact * (1.0 - sigmoid_value))


def place(move):
    group = sum(map(abs, move)) - 1
    return group, GROUPS[group].index(move)


def side_row(move):
    return sum(step * (BS - 1) for step, m in zip(BLOCK_STEPS, move) if m == 1)


def free_axes(move):
    return [axis for axis in range(3) if move[axis] == 0]


def split_lanes(value):
    high = value.astype(jnp.bfloat16).astype(jnp.float32)
    return high + pltpu.roll(value - high, LANES // 2, 1)


def halo_kernel(
    sizes, send_list, preact_far, cotangent_far, active_far, split_grad,
    bias, mask, face_in, edge_in, corner_in, grad, picked, preact, cotangent, active,
    face_out, edge_out, corner_out, send_sem, recv_sem, fetch_sem,
):
    blocks, channels, volume = preact.shape
    listed = send_list.shape[0]
    fetch_active = pltpu.make_async_copy(active_far, active, fetch_sem.at[2 * blocks])
    fetches = [
        [
            pltpu.make_async_copy(far.at[b], near.at[b], fetch_sem.at[2 * b + n])
            for n, (far, near) in enumerate(((preact_far, preact), (cotangent_far, cotangent)))
        ]
        for b in range(blocks)
    ]
    fetch_active.start()
    for fetch in sum(fetches, []):
        fetch.start()
    here = [lax.axis_index(axis) for axis in AXES]

    def inside(move):
        checks = []
        for axis in range(3):
            if move[axis] == 1:
                checks.append((here[axis] < sizes[axis] - 1).astype(jnp.int32))
            elif move[axis] == -1:
                checks.append((here[axis] > 0).astype(jnp.int32))
        return functools.reduce(lambda a, b: a * b, checks)

    live = {move: inside(move) for move in HEADINGS}
    target = {move: tuple(h + m for h, m in zip(here, move)) for move in HEADINGS}
    barrier = pltpu.get_barrier_semaphore()
    for move in HEADINGS:
        @pl.when(live[move] == 1)
        def _():
            pl.semaphore_signal(barrier, inc=1, device_id=target[move], device_id_type=MESH)

    total = jnp.zeros((1, LANES), jnp.float32)
    fetch_active.wait()
    mask[...] = active[...].astype(jnp.float32)
    for b in range(blocks):
        for fetch in fetches[b]:
            fetch.wait()
        value = cotangent[b] * silu_slope(preact[b]) * mask[pl.ds(b, 1), :]
        rows = jnp.concatenate([value, jnp.zeros((LANES - channels, volume), jnp.float32)], axis=0).T
        grad[b] = rows
        total = total + jnp.sum(rows, axis=0, keepdims=True)
    bias[...] = jnp.broadcast_to(total, bias.shape)

    for s in range(listed):
        entry = send_list[s]
        keep = (entry < blocks).astype(jnp.float32)
        picked[...] = grad[jnp.minimum(entry, blocks - 1)] * keep
        for f, move in enumerate(FACES):
            first, second = free_axes(move)
            base = side_row(move)
            tiles = [
                picked[pl.ds(base + u * BLOCK_STEPS[first], BS, stride=BLOCK_STEPS[second]), :]
                for u in range(BS)
            ]
            for u in range(BS // 2):
                face_out[f, s, pl.ds(u * BS, BS), :] = tiles[u] + pltpu.roll(
                    tiles[u + BS // 2], LANES // 2, 1
                )
        for f, move in enumerate(EDGES):
            (along,) = free_axes(move)
            edge_out[f, s] = picked[pl.ds(side_row(move), BS, stride=BLOCK_STEPS[along]), :]
        for f, move in enumerate(CORNERS):
            corner_out[f, s] = jnp.broadcast_to(picked[pl.ds(side_row(move), 1), :], (BS, LANES))

    count = functools.reduce(lambda a, b: a + b, [live[move] for move in HEADINGS])
    pl.semaphore_wait(barrier, count)

    sent, landed = (face_out, edge_out, corner_out), (face_in, edge_in, corner_in)

    def copy_of(move):
        group, f = place(move)
        n = HEADINGS.index(move)
        return pltpu.make_async_remote_copy(
            src_ref=sent[group].at[f],
            dst_ref=landed[group].at[f],
            send_sem=send_sem.at[n],
            recv_sem=recv_sem.at[n],
            device_id=target[move],
            device_id_type=MESH,
        )

    for move in FACES + EDGES + CORNERS:
        @pl.when(live[move] == 1)
        def _():
            copy_of(move).start()

    for b in range(blocks):
        split_grad[b] = split_lanes(grad[b])

    for move in FACES + EDGES + CORNERS:
        back = tuple(-m for m in move)

        @pl.when(live[move] == 1)
        def _():
            copy_of(move).wait_send()

        @pl.when(live[back] == 1)
        def _():
            copy_of(move).wait_recv()


def conv_kernel(
    owner_dir, owner_slot, split_grad, face_in, edge_in, corner_in, features, voxel_mask,
    weights, bias, input_grad, partial, cube, windows, wide, split_weights,
):
    blocks, channels, volume = features.shape
    taps = weights.shape[0]
    for k in range(taps):
        value = weights[k]
        high = value.astype(jnp.bfloat16)
        rest = (value - high.astype(jnp.float32)).astype(jnp.bfloat16)
        column = jnp.concatenate([high, rest], axis=0)
        split_weights[:, pl.ds(k * LANES, LANES)] = jnp.concatenate([column, column], axis=1)
    low_half = lax.broadcasted_iota(jnp.int32, (BS, LANES), 1) < LANES // 2
    wide[...] = jnp.zeros_like(wide)

    def cube_row(move):
        origin = CUBE_STEPS[0] + CUBE_STEPS[1] + BS
        return origin + sum(
            step * (BS if m == 1 else -1) for step, m in zip(CUBE_STEPS, move) if m != 0
        )

    def fill_own(offset, slot):
        back = tuple(-m for m in offset)
        source, into = side_row(back), cube_row(offset)
        free = free_axes(offset)
        if not free:
            cube[pl.ds(into, 1), :] = split_grad[slot, pl.ds(source, 1), :]
            return
        along = free[-1]
        for lead in itertools.product(range(BS), repeat=len(free) - 1):
            shift = sum(BLOCK_STEPS[a] * u for a, u in zip(free, lead))
            move = sum(CUBE_STEPS[a] * u for a, u in zip(free, lead))
            cube[pl.ds(into + move, BS, stride=CUBE_STEPS[along]), :] = split_grad[
                slot, pl.ds(source + shift, BS, stride=BLOCK_STEPS[along]), :
            ]

    def fill_remote(offset, owner, slot):
        group, f = place(tuple(-m for m in owner))
        into = cube_row(offset)
        picks = [BS - 1 if offset[a] == -1 else 0 for a in range(3)]
        if group == 2:
            value = jnp.where(low_half, corner_in[f, slot], 0.0)
            cube[pl.ds(into, 1), :] = split_lanes(value)[:1]
        elif group == 1:
            (along,) = free_axes(owner)
            value = split_lanes(jnp.where(low_half, edge_in[f, slot], 0.0))
            if offset[along] == 0:
                cube[pl.ds(into, BS, stride=CUBE_STEPS[along]), :] = value
            else:
                at = picks[along]
                cube[pl.ds(into, 1), :] = value[at : at + 1]
        else:
            first, second = free_axes(owner)
            for u in range(BS) if offset[first] == 0 else (picks[first],):
                half, row = divmod(u, BS // 2)
                value = face_in[f, slot, pl.ds(row * BS, BS), :]
                if half:
                    value = pltpu.roll(value, LANES // 2, 1)
                value = split_lanes(jnp.where(low_half, value, 0.0))
                at_u = into + (u * CUBE_STEPS[first] if offset[first] == 0 else 0)
                if offset[second] == 0:
                    cube[pl.ds(at_u, BS, stride=CUBE_STEPS[second]), :] = value
                else:
                    at = picks[second]
                    cube[pl.ds(at_u, 1), :] = value[at : at + 1]

    def visit_block(b, carry):
        cube[...] = jnp.zeros_like(cube)
        for x in range(BS):
            for y in range(BS):
                cube[pl.ds(cube_row((0, 0, 0)) + x * CUBE_STEPS[0] + y * CUBE_STEPS[1], BS), :] = (
                    split_grad[b, pl.ds((x * BS + y) * BS, BS), :]
                )
        for offset in HEADINGS:
            o = 9 * (offset[0] + 1) + 3 * (offset[1] + 1) + offset[2] + 1
            code, slot = owner_dir[b, o], owner_slot[b, o]

            @pl.when(code != 27)
            def _():
                @pl.when(code == 13)
                def _():
                    fill_own(offset, slot)

                for owner in itertools.product(*[(0,) if m == 0 else (0, m) for m in offset]):
                    if owner != (0, 0, 0):
                        @pl.when(code == 9 * (owner[0] + 1) + 3 * (owner[1] + 1) + owner[2] + 1)
                        def _():
                            fill_remote(offset, owner, slot)

        for ky in (-1, 0, 1):
            for kz in (-1, 0, 1):
                for x in range(BS + 2):
                    tiles = [
                        cube[pl.ds(x * CUBE_STEPS[0] + (y + 1 - ky) * CUBE_STEPS[1] + BS - kz, BS), :]
                        for y in range(BS)
                    ]
                    windows[3 * (ky + 1) + kz + 1, pl.ds(x * BS * BS, BS * BS), :] = (
                        jnp.concatenate(tiles, axis=0).astype(jnp.bfloat16)
                    )
        whole = jnp.concatenate(
            [
                windows[q, pl.ds((1 - kx) * BS * BS, volume), :]
                for kx in (-1, 0, 1)
                for q in range(9)
            ],
            axis=1,
        )
        mask = voxel_mask[pl.ds(b, 1), :]
        result = lax.dot_general(
            whole, split_weights[...], (((1,), (1,)), ((), ())), preferred_element_type=jnp.float32
        )
        result = (result + pltpu.roll(result, LANES // 2, 1)).T
        input_grad[b] = result[:channels] * mask
        masked = features[b] * mask
        high = masked.astype(jnp.bfloat16)
        rest = (masked - high.astype(jnp.float32)).astype(jnp.bfloat16)
        wide[...] += jnp.dot(
            jnp.concatenate([high, rest], axis=0), whole, preferred_element_type=jnp.float32
        )
        return carry

    lax.fori_loop(0, blocks, visit_block, 0)
    half = lax.broadcasted_iota(jnp.int32, (channels, LANES), 1) < LANES // 2

    def summed(k):
        value = wide[:channels, pl.ds(k * LANES, LANES)] + wide[channels:, pl.ds(k * LANES, LANES)]
        return value + pltpu.roll(value, LANES // 2, 1)

    tiles = channels // BS
    spare = jnp.concatenate(
        [pltpu.roll(bias[...], LANES // 2, 1), jnp.zeros((channels - BS, LANES), jnp.float32)], axis=0
    )
    pairs = (taps + 1) // 2
    for pair in range(pairs):
        value = summed(2 * pair)
        other = summed(2 * pair + 1) if 2 * pair + 1 < taps else spare
        partial[pl.ds(pair * tiles, tiles)] = jnp.where(half, value, other).reshape(tiles, BS, LANES)
    if partial.shape[0] > pairs * tiles:
        rest = partial.shape[0] - pairs * tiles
        partial[pl.ds(pairs * tiles, rest)] = jnp.zeros((rest, BS, LANES), jnp.float32)


def reduce_kernel(
    sizes, chunks, partial, kernel_grad, bias_grad, arrived, line, full,
    near_send, near_recv, line_send, line_recv, back_send, back_recv,
):
    here = [lax.axis_index(axis) for axis in AXES]
    plane, depth = sizes[0] * sizes[1], sizes[2]
    share = partial.shape[0] // (chunks * plane)
    me = here[0] * sizes[1] + here[1]
    peers = [lax.rem(me + j, plane) for j in range(plane)]
    peer_at = [(p // sizes[1], lax.rem(p, sizes[1]), here[2]) for p in peers]
    line_at = [(here[0], here[1], lax.rem(here[2] + j, depth)) for j in range(depth)]
    barrier = pltpu.get_barrier_semaphore()
    for device in peer_at[1:] + line_at[1:]:
        pl.semaphore_signal(barrier, inc=1, device_id=device, device_id_type=MESH)
    pl.semaphore_wait(barrier, plane + depth - 2)

    def part(c, p):
        return pl.ds((c * plane + p) * share, share)

    def scatter(c, j):
        return pltpu.make_async_remote_copy(
            src_ref=partial.at[part(c, peers[j])],
            dst_ref=arrived.at[c, j],
            send_sem=near_send.at[c, j],
            recv_sem=near_recv.at[c, j],
            device_id=peer_at[j],
            device_id_type=MESH,
        )

    def swap(c, j):
        return pltpu.make_async_remote_copy(
            src_ref=line.at[c, here[2]],
            dst_ref=line.at[c, here[2]],
            send_sem=line_send.at[c, j],
            recv_sem=line_recv.at[c, j],
            device_id=line_at[j],
            device_id_type=MESH,
        )

    def gather(c, j):
        return pltpu.make_async_remote_copy(
            src_ref=full.at[part(c, me)],
            dst_ref=full.at[part(c, me)],
            send_sem=back_send.at[c, j],
            recv_sem=back_recv.at[c, j],
            device_id=peer_at[j],
            device_id_type=MESH,
        )

    def landing(c, j):
        behind = lax.rem(me + plane - j, plane)
        return pltpu.make_async_remote_copy(
            src_ref=full.at[part(c, behind)],
            dst_ref=full.at[part(c, behind)],
            send_sem=back_send.at[c, j],
            recv_sem=back_recv.at[c, j],
            device_id=peer_at[j],
            device_id_type=MESH,
        )

    def line_landing(c, j):
        behind = lax.rem(here[2] + depth - j, depth)
        return pltpu.make_async_remote_copy(
            src_ref=line.at[c, behind],
            dst_ref=line.at[c, behind],
            send_sem=line_send.at[c, j],
            recv_sem=line_recv.at[c, j],
            device_id=line_at[j],
            device_id_type=MESH,
        )

    for c in range(chunks):
        for j in range(1, plane):
            scatter(c, j).start()
    for c in range(chunks):
        for j in range(1, plane):
            scatter(c, j).wait_recv()
        total = partial[part(c, me)]
        for j in range(1, plane):
            total = total + arrived[c, j]
        line[c, here[2]] = total
        for j in range(1, depth):
            swap(c, j).start()
    for c in range(chunks):
        for j in range(1, depth):
            line_landing(c, j).wait_recv()
        total = line[c, 0]
        for z in range(1, depth):
            total = total + line[c, z]
        full[part(c, me)] = total
        for j in range(1, plane):
            gather(c, j).start()
    for c in range(chunks):
        for j in range(1, plane):
            landing(c, j).wait_recv()
    taps, channels = kernel_grad.shape[:2]
    tiles = channels // BS
    for pair in range((taps + 1) // 2):
        value = full[pl.ds(pair * tiles, tiles)].reshape(channels, LANES)
        kernel_grad[2 * pair] = value[:, :channels]
        if 2 * pair + 1 < taps:
            kernel_grad[2 * pair + 1] = pltpu.roll(value, LANES // 2, 1)[:, :channels]
        else:
            bias_grad[...] = pltpu.roll(value[:BS], LANES // 2, 1)
    for c in range(chunks):
        for j in range(1, plane):
            scatter(c, j).wait_send()
            gather(c, j).wait_send()
        for j in range(1, depth):
            swap(c, j).wait_send()


def shards(sizes, features, preact, cotangent, kernel, active, owner_dir, owner_slot, send_list):
    blocks, channels, volume = features.shape
    listed = send_list.shape[0]
    taps = kernel.shape[0]
    vmem = pl.BlockSpec(memory_space=pltpu.VMEM)
    smem = pl.BlockSpec(memory_space=pltpu.SMEM)
    shaped = jax.ShapeDtypeStruct
    rows = (BS * BS // 2, BS, BS)
    sheets = [(len(g), listed, r, LANES) for g, r in zip(GROUPS, rows)]
    far = pl.BlockSpec(memory_space=pltpu.HBM)
    split_grad, bias, mask, *landed = pl.pallas_call(
        functools.partial(halo_kernel, sizes),
        out_shape=[
            shaped((blocks, volume, LANES), jnp.float32),
            shaped((BS, LANES), jnp.float32),
            shaped(active.shape, jnp.float32),
        ]
        + [shaped(s, jnp.float32) for s in sheets],
        in_specs=[smem, far, far, far],
        out_specs=[vmem] * 6,
        scratch_shapes=[
            pltpu.VMEM((blocks, volume, LANES), jnp.float32),
            pltpu.VMEM((volume, LANES), jnp.float32),
        ]
        + [pltpu.VMEM(a.shape, a.dtype) for a in (preact, cotangent, active)]
        + [pltpu.VMEM(s, jnp.float32) for s in sheets]
        + [pltpu.SemaphoreType.DMA((len(HEADINGS),))] * 2
        + [pltpu.SemaphoreType.DMA((2 * blocks + 1,))],
        compiler_params=pltpu.CompilerParams(
            collective_id=0, has_side_effects=True, vmem_limit_bytes=20 * 2**20
        ),
        name="halo",
    )(send_list, preact, cotangent, active)
    plane, chunks = sizes[0] * sizes[1], 2
    tiles = (taps + 1) // 2 * channels // BS
    share = -(-tiles // (plane * chunks))
    tiles = share * plane * chunks
    input_grad, partial = pl.pallas_call(
        conv_kernel,
        out_shape=[
            shaped((blocks, channels, volume), jnp.float32),
            shaped((tiles, BS, LANES), jnp.float32),
        ],
        in_specs=[smem, smem] + [vmem] * 8,
        out_specs=[vmem] * 2,
        scratch_shapes=[
            pltpu.VMEM(((BS + 2) * CUBE_STEPS[0], LANES), jnp.float32),
            pltpu.VMEM((9, (BS + 2) * BS * BS, LANES), jnp.bfloat16),
            pltpu.VMEM((2 * channels, taps * LANES), jnp.float32),
            pltpu.VMEM((2 * channels, taps * LANES), jnp.bfloat16),
        ],
        compiler_params=pltpu.CompilerParams(vmem_limit_bytes=32 * 2**20),
        name="conv",
    )(owner_dir, owner_slot, split_grad, *landed, features, mask, kernel, bias)
    total, bias_total = pl.pallas_call(
        functools.partial(reduce_kernel, sizes, chunks),
        out_shape=[shaped(kernel.shape, jnp.float32), shaped((BS, LANES), jnp.float32)],
        in_specs=[vmem],
        out_specs=[vmem] * 2,
        scratch_shapes=[
            pltpu.VMEM((chunks, plane, share, BS, LANES), jnp.float32),
            pltpu.VMEM((chunks, sizes[2], share, BS, LANES), jnp.float32),
            pltpu.VMEM((tiles, BS, LANES), jnp.float32),
        ]
        + [pltpu.SemaphoreType.DMA((chunks, n)) for n in (plane, plane, sizes[2], sizes[2], plane, plane)],
        compiler_params=pltpu.CompilerParams(
            collective_id=1, has_side_effects=True, vmem_limit_bytes=20 * 2**20
        ),
        name="reduce",
    )(partial)
    scaling = (volume * blocks * lax.axis_size(AXES)) ** (-0.5)
    return input_grad, total * scaling, bias_total[0, :channels] * scaling


def solution(mesh):
    whole = P(AXES, None, None)
    table = P(AXES, None)
    sizes = tuple(mesh.shape[axis] for axis in AXES)
    return jax.shard_map(
        functools.partial(shards, sizes),
        mesh=mesh,
        in_specs=(whole, whole, whole, P(), table, table, table, P(AXES)),
        out_specs=(whole, P(), P()),
        check_vma=False,
    )
```

```python
import functools
import itertools
import math

import jax
import jax.numpy as jnp
from jax import lax
from jax.experimental import pallas as pl
from jax.experimental.pallas import tpu as pltpu
from jax.sharding import PartitionSpec as P

BS = 8
LANES = 128
AXES = ("gx", "gy", "gz")
MESH = pl.DeviceIdType.MESH
DEPTH = 3 * BS
CUBE_STEPS = ((BS + 2) * DEPTH, DEPTH, 1)
BLOCK_STEPS = (BS * BS, BS, 1)
HEADINGS = [m for m in itertools.product((-1, 0, 1), repeat=3) if m != (0, 0, 0)]
FACES = [m for m in HEADINGS if sum(map(abs, m)) == 1]
EDGES = [m for m in HEADINGS if sum(map(abs, m)) == 2]
CORNERS = [m for m in HEADINGS if sum(map(abs, m)) == 3]
GROUPS = (FACES, EDGES, CORNERS)


def silu_slope(preact):
    sigmoid_value = jax.nn.sigmoid(preact)
    return sigmoid_value * (1.0 + preact * (1.0 - sigmoid_value))


def place(move):
    group = sum(map(abs, move)) - 1
    return group, GROUPS[group].index(move)


def side_row(move):
    return sum(step * (BS - 1) for step, m in zip(BLOCK_STEPS, move) if m == 1)


def free_axes(move):
    return [axis for axis in range(3) if move[axis] == 0]


def split_lanes(value):
    high = value.astype(jnp.bfloat16).astype(jnp.float32)
    return high + pltpu.roll(value - high, LANES // 2, 1)


def halo_kernel(
    sizes, send_list, preact_far, cotangent_far, active_far, split_grad,
    bias, mask, face_in, edge_in, corner_in, grad, picked, preact, cotangent, active,
    face_out, edge_out, corner_out, send_sem, recv_sem, fetch_sem,
):
    blocks, channels, volume = preact.shape
    listed = send_list.shape[0]
    fetch_active = pltpu.make_async_copy(active_far, active, fetch_sem.at[2 * blocks])
    fetches = [
        [
            pltpu.make_async_copy(far.at[b], near.at[b], fetch_sem.at[2 * b + n])
            for n, (far, near) in enumerate(((preact_far, preact), (cotangent_far, cotangent)))
        ]
        for b in range(blocks)
    ]
    fetch_active.start()
    for fetch in sum(fetches, []):
        fetch.start()
    here = [lax.axis_index(axis) for axis in AXES]

    def inside(move):
        checks = []
        for axis in range(3):
            if move[axis] == 1:
                checks.append((here[axis] < sizes[axis] - 1).astype(jnp.int32))
            elif move[axis] == -1:
                checks.append((here[axis] > 0).astype(jnp.int32))
        return functools.reduce(lambda a, b: a * b, checks)

    live = {move: inside(move) for move in HEADINGS}
    target = {move: tuple(h + m for h, m in zip(here, move)) for move in HEADINGS}
    barrier = pltpu.get_barrier_semaphore()
    for move in HEADINGS:
        @pl.when(live[move] == 1)
        def _():
            pl.semaphore_signal(barrier, inc=1, device_id=target[move], device_id_type=MESH)

    total = jnp.zeros((1, LANES), jnp.float32)
    fetch_active.wait()
    mask[...] = active[...].astype(jnp.float32)
    for b in range(blocks):
        for fetch in fetches[b]:
            fetch.wait()
        value = cotangent[b] * silu_slope(preact[b]) * mask[pl.ds(b, 1), :]
        rows = jnp.concatenate([value, jnp.zeros((LANES - channels, volume), jnp.float32)], axis=0).T
        grad[b] = rows
        total = total + jnp.sum(rows, axis=0, keepdims=True)
    bias[...] = jnp.broadcast_to(total, bias.shape)

    for s in range(listed):
        entry = send_list[s]
        keep = (entry < blocks).astype(jnp.float32)
        picked[...] = grad[jnp.minimum(entry, blocks - 1)] * keep
        for f, move in enumerate(FACES):
            first, second = free_axes(move)
            base = side_row(move)
            tiles = [
                picked[pl.ds(base + u * BLOCK_STEPS[first], BS, stride=BLOCK_STEPS[second]), :]
                for u in range(BS)
            ]
            for u in range(BS // 2):
                face_out[f, s, pl.ds(u * BS, BS), :] = tiles[u] + pltpu.roll(
                    tiles[u + BS // 2], LANES // 2, 1
                )
        for f, move in enumerate(EDGES):
            (along,) = free_axes(move)
            edge_out[f, s] = picked[pl.ds(side_row(move), BS, stride=BLOCK_STEPS[along]), :]
        for f, move in enumerate(CORNERS):
            corner_out[f, s] = jnp.broadcast_to(picked[pl.ds(side_row(move), 1), :], (BS, LANES))

    count = functools.reduce(lambda a, b: a + b, [live[move] for move in HEADINGS])
    pl.semaphore_wait(barrier, count)

    sent, landed = (face_out, edge_out, corner_out), (face_in, edge_in, corner_in)

    def copy_of(move):
        group, f = place(move)
        n = HEADINGS.index(move)
        return pltpu.make_async_remote_copy(
            src_ref=sent[group].at[f],
            dst_ref=landed[group].at[f],
            send_sem=send_sem.at[n],
            recv_sem=recv_sem.at[n],
            device_id=target[move],
            device_id_type=MESH,
        )

    for move in FACES + EDGES + CORNERS:
        @pl.when(live[move] == 1)
        def _():
            copy_of(move).start()

    for b in range(blocks):
        split_grad[b] = split_lanes(grad[b])

    for move in FACES + EDGES + CORNERS:
        back = tuple(-m for m in move)

        @pl.when(live[move] == 1)
        def _():
            copy_of(move).wait_send()

        @pl.when(live[back] == 1)
        def _():
            copy_of(move).wait_recv()


def window_kernel(
    owner_dir, owner_slot, split_grad, face_in, edge_in, corner_in, windows, cube
):
    blocks = split_grad.shape[0]
    low_half = lax.broadcasted_iota(jnp.int32, (BS, LANES), 1) < LANES // 2

    def cube_row(move):
        origin = CUBE_STEPS[0] + CUBE_STEPS[1] + BS
        return origin + sum(
            step * (BS if m == 1 else -1) for step, m in zip(CUBE_STEPS, move) if m != 0
        )

    def fill_own(offset, slot):
        back = tuple(-m for m in offset)
        source, into = side_row(back), cube_row(offset)
        free = free_axes(offset)
        if not free:
            cube[pl.ds(into, 1), :] = split_grad[slot, pl.ds(source, 1), :]
            return
        along = free[-1]
        for lead in itertools.product(range(BS), repeat=len(free) - 1):
            shift = sum(BLOCK_STEPS[a] * u for a, u in zip(free, lead))
            move = sum(CUBE_STEPS[a] * u for a, u in zip(free, lead))
            cube[pl.ds(into + move, BS, stride=CUBE_STEPS[along]), :] = split_grad[
                slot, pl.ds(source + shift, BS, stride=BLOCK_STEPS[along]), :
            ]

    def fill_remote(offset, owner, slot):
        group, f = place(tuple(-m for m in owner))
        into = cube_row(offset)
        picks = [BS - 1 if offset[a] == -1 else 0 for a in range(3)]
        if group == 2:
            value = jnp.where(low_half, corner_in[f, slot], 0.0)
            cube[pl.ds(into, 1), :] = split_lanes(value)[:1]
        elif group == 1:
            (along,) = free_axes(owner)
            value = split_lanes(jnp.where(low_half, edge_in[f, slot], 0.0))
            if offset[along] == 0:
                cube[pl.ds(into, BS, stride=CUBE_STEPS[along]), :] = value
            else:
                at = picks[along]
                cube[pl.ds(into, 1), :] = value[at : at + 1]
        else:
            first, second = free_axes(owner)
            for u in range(BS) if offset[first] == 0 else (picks[first],):
                half, row = divmod(u, BS // 2)
                value = face_in[f, slot, pl.ds(row * BS, BS), :]
                if half:
                    value = pltpu.roll(value, LANES // 2, 1)
                value = split_lanes(jnp.where(low_half, value, 0.0))
                at_u = into + (u * CUBE_STEPS[first] if offset[first] == 0 else 0)
                if offset[second] == 0:
                    cube[pl.ds(at_u, BS, stride=CUBE_STEPS[second]), :] = value
                else:
                    at = picks[second]
                    cube[pl.ds(at_u, 1), :] = value[at : at + 1]

    def visit_block(b, carry):
        cube[...] = jnp.zeros_like(cube)
        for x in range(BS):
            for y in range(BS):
                cube[pl.ds(cube_row((0, 0, 0)) + x * CUBE_STEPS[0] + y * CUBE_STEPS[1], BS), :] = (
                    split_grad[b, pl.ds((x * BS + y) * BS, BS), :]
                )
        for offset in HEADINGS:
            o = 9 * (offset[0] + 1) + 3 * (offset[1] + 1) + offset[2] + 1
            code, slot = owner_dir[b, o], owner_slot[b, o]

            @pl.when(code != 27)
            def _():
                @pl.when(code == 13)
                def _():
                    fill_own(offset, slot)

                for owner in itertools.product(*[(0,) if m == 0 else (0, m) for m in offset]):
                    if owner != (0, 0, 0):
                        @pl.when(code == 9 * (owner[0] + 1) + 3 * (owner[1] + 1) + owner[2] + 1)
                        def _():
                            fill_remote(offset, owner, slot)

        for ky in (-1, 0, 1):
            for kz in (-1, 0, 1):
                for x in range(BS + 2):
                    tiles = [
                        cube[pl.ds(x * CUBE_STEPS[0] + (y + 1 - ky) * CUBE_STEPS[1] + BS - kz, BS), :]
                        for y in range(BS)
                    ]
                    windows[b, 3 * (ky + 1) + kz + 1, pl.ds(x * BS * BS, BS * BS), :] = (
                        jnp.concatenate(tiles, axis=0).astype(jnp.bfloat16)
                    )
        return carry

    lax.fori_loop(0, blocks, visit_block, 0)


def window(windows, b, k, volume):
    kx, q = divmod(k, 9)
    return windows[b, q, pl.ds((2 - kx) * BS * BS, volume), :]


def conv_kernel(
    sizes, chunks, windows, features, voxel_mask, weights, bias, input_grad, kernel_grad, bias_grad,
    partial, full, split_weights, split_input, *rest,
):
    blocks, channels, volume = features.shape
    taps = weights.shape[0]
    here = [lax.axis_index(axis) for axis in AXES]
    groups = stage_sizes(sizes)
    stages = len(groups)
    arrived, sums, sems = rest[:stages], rest[stages : 2 * stages], rest[2 * stages :]
    pair = groups[0]
    column, low = here[0] // pair, lax.rem(here[0], pair)
    mine = (low, column * sizes[1] + here[1], here[2])

    def member(g, j):
        p = lax.rem(mine[g] + j, groups[g])
        if g == 0:
            return p, (column * pair + p, here[1], here[2])
        if g == 1:
            return p, (p // sizes[1] * pair + low, lax.rem(p, sizes[1]), here[2])
        return p, (here[0], here[1], p)

    lengths = [full.shape[1]]
    for n in groups:
        lengths.append(lengths[-1] // n)
    bases = [0]
    for g in range(stages):
        bases.append(bases[-1] + mine[g] * lengths[g + 1])

    barrier = pltpu.get_barrier_semaphore()
    for g, n in enumerate(groups):
        for j in range(1, n):
            pl.semaphore_signal(barrier, inc=1, device_id=member(g, j)[1], device_id_type=MESH)

    def scatter(c, g, j):
        p, device = member(g, j)
        source = partial.at[c] if g == 0 else sums[g - 1].at[c]
        return pltpu.make_async_remote_copy(
            src_ref=source.at[pl.ds(p * lengths[g + 1], lengths[g + 1])],
            dst_ref=arrived[g].at[c, j],
            send_sem=sems[4 * g].at[c, j],
            recv_sem=sems[4 * g + 1].at[c, j],
            device_id=device,
            device_id_type=MESH,
        )

    def gather(c, g, j, place_of):
        area = full.at[c, pl.ds(bases[g] + place_of * lengths[g + 1], lengths[g + 1])]
        return pltpu.make_async_remote_copy(
            src_ref=area,
            dst_ref=area,
            send_sem=sems[4 * g + 2].at[c, j],
            recv_sem=sems[4 * g + 3].at[c, j],
            device_id=member(g, j)[1],
            device_id_type=MESH,
        )

    def start_scatter(c, g):
        for j in range(1, groups[g]):
            scatter(c, g, j).start()

    def finish_scatter(c, g):
        for j in range(1, groups[g]):
            scatter(c, g, j).wait_recv()
        own = pl.ds(mine[g] * lengths[g + 1], lengths[g + 1])
        total = partial[c, own] if g == 0 else sums[g - 1][c, own]
        for j in range(1, groups[g]):
            total = total + arrived[g][c, j]
        if g + 1 < stages:
            sums[g][c] = total
        else:
            full[c, pl.ds(bases[stages], lengths[stages])] = total

    def start_gather(c, g):
        for j in range(1, groups[g]):
            gather(c, g, j, mine[g]).start()

    def finish_gather(c, g):
        for j in range(1, groups[g]):
            gather(c, g, j, lax.rem(mine[g] + groups[g] - j, groups[g])).wait_recv()

    half = lax.broadcasted_iota(jnp.int32, (channels, LANES), 1) < LANES // 2
    tiles = channels // BS
    pairs = (taps + 1) // 2
    per_chunk = full.shape[1] // tiles

    for b in range(blocks):
        masked = features[b] * voxel_mask[pl.ds(b, 1), :]
        high = masked.astype(jnp.bfloat16)
        low_part = (masked - high.astype(jnp.float32)).astype(jnp.bfloat16)
        split_input[:, pl.ds(b * volume, volume)] = jnp.concatenate([high, low_part], axis=0)

    def tap_pair(n):
        span = [k for k in (2 * n, 2 * n + 1) if k < taps]
        rows = jnp.concatenate(
            [
                jnp.concatenate([window(windows, b, k, volume) for k in span], axis=1)
                for b in range(blocks)
            ],
            axis=0,
        )
        wide = jnp.dot(split_input[...], rows, preferred_element_type=jnp.float32)
        wide = wide[:channels] + wide[channels:]
        parts = [wide[:, m * LANES : (m + 1) * LANES] for m in range(len(span))]
        parts = [v + pltpu.roll(v, LANES // 2, 1) for v in parts]
        if len(parts) == 1:
            spare = jnp.zeros((channels - BS, LANES), jnp.float32)
            parts.append(
                jnp.concatenate([pltpu.roll(bias[...], LANES // 2, 1), spare], axis=0)
            )
        return jnp.where(half, *parts).reshape(tiles, BS, LANES)

    def products(c):
        for m in range(per_chunk):
            n = c * per_chunk + m
            partial[c, pl.ds(m * tiles, tiles)] = (
                tap_pair(n) if n < pairs else jnp.zeros((tiles, BS, LANES), jnp.float32)
            )

    def input_block(b):
        whole = jnp.concatenate([window(windows, b, k, volume) for k in range(taps)], axis=1)
        result = lax.dot_general(
            whole, split_weights[...], (((1,), (1,)), ((), ())), preferred_element_type=jnp.float32
        )
        result = (result + pltpu.roll(result, LANES // 2, 1)).T
        input_grad[b] = result[:channels] * voxel_mask[pl.ds(b, 1), :]

    products(0)
    pl.semaphore_wait(barrier, sum(groups) - stages)
    start_scatter(0, 0)
    for c in range(1, chunks):
        products(c)
        start_scatter(c, 0)

    def prepare_weights():
        for k in range(taps):
            value = weights[k]
            high = value.astype(jnp.bfloat16)
            low_part = (value - high.astype(jnp.float32)).astype(jnp.bfloat16)
            line = jnp.concatenate([high, low_part], axis=0)
            split_weights[:, pl.ds(k * LANES, LANES)] = jnp.concatenate([line, line], axis=1)

    queue = [prepare_weights] + [functools.partial(input_block, b) for b in range(blocks)]
    for g in range(stages):
        for c in range(chunks):
            finish_scatter(c, g)
            start_scatter(c, g + 1) if g + 1 < stages else start_gather(c, g)
        for _ in range(2):
            if queue:
                queue.pop(0)()
    for g in reversed(range(stages)):
        for c in range(chunks):
            finish_gather(c, g)
            if g:
                start_gather(c, g - 1)
        if queue:
            queue.pop(0)()
    for work in queue:
        work()

    for n in range(pairs):
        c, m = divmod(n, per_chunk)
        value = full[c, pl.ds(m * tiles, tiles)].reshape(channels, LANES)
        kernel_grad[2 * n] = value[:, :channels]
        if 2 * n + 1 < taps:
            kernel_grad[2 * n + 1] = pltpu.roll(value, LANES // 2, 1)[:, :channels]
        else:
            bias_grad[...] = pltpu.roll(value[:BS], LANES // 2, 1)
    for g in range(stages):
        for c in range(chunks):
            for j in range(1, groups[g]):
                scatter(c, g, j).wait_send()
                gather(c, g, j, mine[g]).wait_send()


def stage_sizes(sizes):
    pair = 2 if sizes[0] % 2 == 0 else 1
    return pair, sizes[0] // pair * sizes[1], sizes[2]


def shards(sizes, features, preact, cotangent, kernel, active, owner_dir, owner_slot, send_list):
    blocks, channels, volume = features.shape
    listed = send_list.shape[0]
    taps = kernel.shape[0]
    vmem = pl.BlockSpec(memory_space=pltpu.VMEM)
    smem = pl.BlockSpec(memory_space=pltpu.SMEM)
    shaped = jax.ShapeDtypeStruct
    rows = (BS * BS // 2, BS, BS)
    sheets = [(len(g), listed, r, LANES) for g, r in zip(GROUPS, rows)]
    far = pl.BlockSpec(memory_space=pltpu.HBM)
    split_grad, bias, mask, *landed = pl.pallas_call(
        functools.partial(halo_kernel, sizes),
        out_shape=[
            shaped((blocks, volume, LANES), jnp.float32),
            shaped((BS, LANES), jnp.float32),
            shaped(active.shape, jnp.float32),
        ]
        + [shaped(s, jnp.float32) for s in sheets],
        in_specs=[smem, far, far, far],
        out_specs=[vmem] * 6,
        scratch_shapes=[
            pltpu.VMEM((blocks, volume, LANES), jnp.float32),
            pltpu.VMEM((volume, LANES), jnp.float32),
        ]
        + [pltpu.VMEM(a.shape, a.dtype) for a in (preact, cotangent, active)]
        + [pltpu.VMEM(s, jnp.float32) for s in sheets]
        + [pltpu.SemaphoreType.DMA((len(HEADINGS),))] * 2
        + [pltpu.SemaphoreType.DMA((2 * blocks + 1,))],
        compiler_params=pltpu.CompilerParams(
            collective_id=0, has_side_effects=True, vmem_limit_bytes=20 * 2**20
        ),
        name="halo",
    )(send_list, preact, cotangent, active)
    windows = pl.pallas_call(
        window_kernel,
        out_shape=shaped((blocks, 9, (BS + 2) * BS * BS, LANES), jnp.bfloat16),
        in_specs=[smem, smem] + [vmem] * 4,
        out_specs=vmem,
        scratch_shapes=[pltpu.VMEM(((BS + 2) * CUBE_STEPS[0], LANES), jnp.float32)],
        compiler_params=pltpu.CompilerParams(vmem_limit_bytes=20 * 2**20),
        name="windows",
    )(owner_dir, owner_slot, split_grad, *landed)
    groups, chunks = stage_sizes(sizes), 2
    pair_tiles = channels // BS
    step = chunks * math.lcm(math.prod(groups), pair_tiles)
    tiles = -(-((taps + 1) // 2 * pair_tiles) // step) * step // chunks
    lengths = [tiles]
    for n in groups:
        lengths.append(lengths[-1] // n)
    input_grad, total, bias_total = pl.pallas_call(
        functools.partial(conv_kernel, sizes, chunks),
        out_shape=[
            shaped(features.shape, jnp.float32),
            shaped(kernel.shape, jnp.float32),
            shaped((BS, LANES), jnp.float32),
        ],
        in_specs=[vmem] * 5,
        out_specs=[vmem] * 3,
        scratch_shapes=[
            pltpu.VMEM((chunks, tiles, BS, LANES), jnp.float32),
            pltpu.VMEM((chunks, tiles, BS, LANES), jnp.float32),
            pltpu.VMEM((2 * channels, taps * LANES), jnp.bfloat16),
            pltpu.VMEM((2 * channels, blocks * volume), jnp.bfloat16),
        ]
        + [pltpu.VMEM((chunks, n, m, BS, LANES), jnp.float32) for n, m in zip(groups, lengths[1:])]
        + [pltpu.VMEM((chunks, m, BS, LANES), jnp.float32) for m in lengths[1:]]
        + [pltpu.SemaphoreType.DMA((chunks, n)) for n in groups for _ in range(4)],
        compiler_params=pltpu.CompilerParams(
            collective_id=1, has_side_effects=True, vmem_limit_bytes=32 * 2**20
        ),
        name="conv",
    )(windows, features, mask, kernel, bias)
    scaling = (volume * blocks * lax.axis_size(AXES)) ** (-0.5)
    return input_grad, total * scaling, bias_total[0, :channels] * scaling


def solution(mesh):
    whole = P(AXES, None, None)
    table = P(AXES, None)
    sizes = tuple(mesh.shape[axis] for axis in AXES)
    return jax.shard_map(
        functools.partial(shards, sizes),
        mesh=mesh,
        in_specs=(whole, whole, whole, P(), table, table, table, P(AXES)),
        out_specs=(whole, P(), P()),
        check_vma=False,
    )
```

```python
import functools
import itertools
import math

import jax
import jax.numpy as jnp
from jax import lax
from jax.experimental import pallas as pl
from jax.experimental.pallas import tpu as pltpu
from jax.sharding import PartitionSpec as P

BS = 8
LANES = 128
AXES = ("gx", "gy", "gz")
MESH = pl.DeviceIdType.MESH
DEPTH = 3 * BS
CUBE_STEPS = ((BS + 2) * DEPTH, DEPTH, 1)
BLOCK_STEPS = (BS * BS, BS, 1)
HEADINGS = [m for m in itertools.product((-1, 0, 1), repeat=3) if m != (0, 0, 0)]
FACES = [m for m in HEADINGS if sum(map(abs, m)) == 1]
EDGES = [m for m in HEADINGS if sum(map(abs, m)) == 2]
CORNERS = [m for m in HEADINGS if sum(map(abs, m)) == 3]
GROUPS = (FACES, EDGES, CORNERS)


def silu_slope(preact):
    sigmoid_value = jax.nn.sigmoid(preact)
    return sigmoid_value * (1.0 + preact * (1.0 - sigmoid_value))


def place(move):
    group = sum(map(abs, move)) - 1
    return group, GROUPS[group].index(move)


def side_row(move):
    return sum(step * (BS - 1) for step, m in zip(BLOCK_STEPS, move) if m == 1)


def free_axes(move):
    return [axis for axis in range(3) if move[axis] == 0]


def split_lanes(value):
    high = value.astype(jnp.bfloat16).astype(jnp.float32)
    return high + pltpu.roll(value - high, LANES // 2, 1)


def halo_kernel(
    sizes, send_list, preact_far, cotangent_far, active_far, split_grad,
    bias, mask, face_in, edge_in, corner_in, grad, picked, preact, cotangent, active,
    face_out, edge_out, corner_out, send_sem, recv_sem, fetch_sem,
):
    blocks, channels, volume = preact.shape
    listed = send_list.shape[0]
    fetch_active = pltpu.make_async_copy(active_far, active, fetch_sem.at[2 * blocks])
    fetches = [
        [
            pltpu.make_async_copy(far.at[b], near.at[b], fetch_sem.at[2 * b + n])
            for n, (far, near) in enumerate(((preact_far, preact), (cotangent_far, cotangent)))
        ]
        for b in range(blocks)
    ]
    fetch_active.start()
    for fetch in sum(fetches, []):
        fetch.start()
    here = [lax.axis_index(axis) for axis in AXES]

    def inside(move):
        checks = []
        for axis in range(3):
            if move[axis] == 1:
                checks.append((here[axis] < sizes[axis] - 1).astype(jnp.int32))
            elif move[axis] == -1:
                checks.append((here[axis] > 0).astype(jnp.int32))
        return functools.reduce(lambda a, b: a * b, checks)

    live = {move: inside(move) for move in HEADINGS}
    target = {move: tuple(h + m for h, m in zip(here, move)) for move in HEADINGS}
    barrier = pltpu.get_barrier_semaphore()
    for move in HEADINGS:
        @pl.when(live[move] == 1)
        def _():
            pl.semaphore_signal(barrier, inc=1, device_id=target[move], device_id_type=MESH)

    total = jnp.zeros((1, LANES), jnp.float32)
    fetch_active.wait()
    mask[...] = active[...].astype(jnp.float32)
    for b in range(blocks):
        for fetch in fetches[b]:
            fetch.wait()
        value = cotangent[b] * silu_slope(preact[b]) * mask[pl.ds(b, 1), :]
        rows = jnp.concatenate([value, jnp.zeros((LANES - channels, volume), jnp.float32)], axis=0).T
        grad[b] = rows
        total = total + jnp.sum(rows, axis=0, keepdims=True)
    bias[...] = jnp.broadcast_to(total, bias.shape)

    corner_out[...] = jnp.zeros_like(corner_out)
    for s in range(listed):
        entry = send_list[s]
        keep = (entry < blocks).astype(jnp.float32)
        picked[...] = grad[jnp.minimum(entry, blocks - 1)] * keep
        for f, move in enumerate(FACES):
            first, second = free_axes(move)
            base = side_row(move)
            tiles = [
                picked[pl.ds(base + u * BLOCK_STEPS[first], BS, stride=BLOCK_STEPS[second]), :]
                for u in range(BS)
            ]
            for u in range(BS // 2):
                face_out[f, s, pl.ds(u * BS, BS), :] = tiles[u] + pltpu.roll(
                    tiles[u + BS // 2], LANES // 2, 1
                )
        for f, move in enumerate(EDGES):
            (along,) = free_axes(move)
            edge_out[f, s] = picked[pl.ds(side_row(move), BS, stride=BLOCK_STEPS[along]), :]
        for f, move in enumerate(CORNERS):
            corner_out[f, pl.ds(s, 1), :] = picked[pl.ds(side_row(move), 1), :]

    count = functools.reduce(lambda a, b: a + b, [live[move] for move in HEADINGS])
    pl.semaphore_wait(barrier, count)

    sent, landed = (face_out, edge_out, corner_out), (face_in, edge_in, corner_in)

    def copy_of(move):
        group, f = place(move)
        n = HEADINGS.index(move)
        return pltpu.make_async_remote_copy(
            src_ref=sent[group].at[f],
            dst_ref=landed[group].at[f],
            send_sem=send_sem.at[n],
            recv_sem=recv_sem.at[n],
            device_id=target[move],
            device_id_type=MESH,
        )

    for move in FACES + EDGES + CORNERS:
        @pl.when(live[move] == 1)
        def _():
            copy_of(move).start()

    for b in range(blocks):
        split_grad[b] = split_lanes(grad[b])

    for move in FACES + EDGES + CORNERS:
        back = tuple(-m for m in move)

        @pl.when(live[move] == 1)
        def _():
            copy_of(move).wait_send()

        @pl.when(live[back] == 1)
        def _():
            copy_of(move).wait_recv()


def window_kernel(
    owner_dir, owner_slot, split_grad, face_in, edge_in, corner_in, windows, cube
):
    blocks = split_grad.shape[0]
    low_half = lax.broadcasted_iota(jnp.int32, (BS, LANES), 1) < LANES // 2

    def cube_row(move):
        origin = CUBE_STEPS[0] + CUBE_STEPS[1] + BS
        return origin + sum(
            step * (BS if m == 1 else -1) for step, m in zip(CUBE_STEPS, move) if m != 0
        )

    def fill_own(offset, slot):
        back = tuple(-m for m in offset)
        source, into = side_row(back), cube_row(offset)
        free = free_axes(offset)
        if not free:
            cube[pl.ds(into, 1), :] = split_grad[slot, pl.ds(source, 1), :]
            return
        along = free[-1]
        for lead in itertools.product(range(BS), repeat=len(free) - 1):
            shift = sum(BLOCK_STEPS[a] * u for a, u in zip(free, lead))
            move = sum(CUBE_STEPS[a] * u for a, u in zip(free, lead))
            cube[pl.ds(into + move, BS, stride=CUBE_STEPS[along]), :] = split_grad[
                slot, pl.ds(source + shift, BS, stride=BLOCK_STEPS[along]), :
            ]

    def fill_remote(offset, owner, slot):
        group, f = place(tuple(-m for m in owner))
        into = cube_row(offset)
        picks = [BS - 1 if offset[a] == -1 else 0 for a in range(3)]
        if group == 2:
            value = jnp.where(low_half[:1], corner_in[f, pl.ds(slot, 1), :], 0.0)
            cube[pl.ds(into, 1), :] = split_lanes(value)
        elif group == 1:
            (along,) = free_axes(owner)
            value = split_lanes(jnp.where(low_half, edge_in[f, slot], 0.0))
            if offset[along] == 0:
                cube[pl.ds(into, BS, stride=CUBE_STEPS[along]), :] = value
            else:
                at = picks[along]
                cube[pl.ds(into, 1), :] = value[at : at + 1]
        else:
            first, second = free_axes(owner)
            for u in range(BS) if offset[first] == 0 else (picks[first],):
                half, row = divmod(u, BS // 2)
                value = face_in[f, slot, pl.ds(row * BS, BS), :]
                if half:
                    value = pltpu.roll(value, LANES // 2, 1)
                value = split_lanes(jnp.where(low_half, value, 0.0))
                at_u = into + (u * CUBE_STEPS[first] if offset[first] == 0 else 0)
                if offset[second] == 0:
                    cube[pl.ds(at_u, BS, stride=CUBE_STEPS[second]), :] = value
                else:
                    at = picks[second]
                    cube[pl.ds(at_u, 1), :] = value[at : at + 1]

    def visit_block(b, carry):
        cube[...] = jnp.zeros_like(cube)
        for x in range(BS):
            for y in range(BS):
                cube[pl.ds(cube_row((0, 0, 0)) + x * CUBE_STEPS[0] + y * CUBE_STEPS[1], BS), :] = (
                    split_grad[b, pl.ds((x * BS + y) * BS, BS), :]
                )
        for offset in HEADINGS:
            o = 9 * (offset[0] + 1) + 3 * (offset[1] + 1) + offset[2] + 1
            code, slot = owner_dir[b, o], owner_slot[b, o]

            @pl.when(code != 27)
            def _():
                @pl.when(code == 13)
                def _():
                    fill_own(offset, slot)

                for owner in itertools.product(*[(0,) if m == 0 else (0, m) for m in offset]):
                    if owner != (0, 0, 0):
                        @pl.when(code == 9 * (owner[0] + 1) + 3 * (owner[1] + 1) + owner[2] + 1)
                        def _():
                            fill_remote(offset, owner, slot)

        for ky in (-1, 0, 1):
            for kz in (-1, 0, 1):
                for x in range(BS + 2):
                    tiles = [
                        cube[pl.ds(x * CUBE_STEPS[0] + (y + 1 - ky) * CUBE_STEPS[1] + BS - kz, BS), :]
                        for y in range(BS)
                    ]
                    windows[b, 3 * (ky + 1) + kz + 1, pl.ds(x * BS * BS, BS * BS), :] = (
                        jnp.concatenate(tiles, axis=0).astype(jnp.bfloat16)
                    )
        return carry

    lax.fori_loop(0, blocks, visit_block, 0)


def window(windows, b, k, volume):
    kx, q = divmod(k, 9)
    return windows[b, q, pl.ds((2 - kx) * BS * BS, volume), :]


def conv_kernel(
    sizes, chunks, windows, features, voxel_mask, weights, bias, input_grad, full,
    partial, split_weights, split_input, *rest,
):
    blocks, channels, volume = features.shape
    taps = weights.shape[0]
    here = [lax.axis_index(axis) for axis in AXES]
    groups = stage_sizes(sizes)
    stages = len(groups)
    arrived, sums, sems = rest[:stages], rest[stages : 2 * stages], rest[2 * stages :]
    pair = groups[0]
    column, low = here[0] // pair, lax.rem(here[0], pair)
    mine = (low, column * sizes[1] + here[1], here[2])

    def member(g, j):
        p = lax.rem(mine[g] + j, groups[g])
        if g == 0:
            return p, (column * pair + p, here[1], here[2])
        if g == 1:
            return p, (p // sizes[1] * pair + low, lax.rem(p, sizes[1]), here[2])
        return p, (here[0], here[1], p)

    lengths = [full.shape[1]]
    for n in groups:
        lengths.append(lengths[-1] // n)
    bases = [0]
    for g in range(stages):
        bases.append(bases[-1] + mine[g] * lengths[g + 1])

    barrier = pltpu.get_barrier_semaphore()
    for g, n in enumerate(groups):
        for j in range(1, n):
            pl.semaphore_signal(barrier, inc=1, device_id=member(g, j)[1], device_id_type=MESH)

    def scatter(c, g, j):
        p, device = member(g, j)
        source = partial.at[c] if g == 0 else sums[g - 1].at[c]
        return pltpu.make_async_remote_copy(
            src_ref=source.at[pl.ds(p * lengths[g + 1], lengths[g + 1])],
            dst_ref=arrived[g].at[c, j],
            send_sem=sems[4 * g].at[c, j],
            recv_sem=sems[4 * g + 1].at[c, j],
            device_id=device,
            device_id_type=MESH,
        )

    def gather(c, g, j, place_of):
        area = full.at[c, pl.ds(bases[g] + place_of * lengths[g + 1], lengths[g + 1])]
        return pltpu.make_async_remote_copy(
            src_ref=area,
            dst_ref=area,
            send_sem=sems[4 * g + 2].at[c, j],
            recv_sem=sems[4 * g + 3].at[c, j],
            device_id=member(g, j)[1],
            device_id_type=MESH,
        )

    def start_scatter(c, g):
        for j in range(1, groups[g]):
            scatter(c, g, j).start()

    def finish_scatter(c, g):
        for j in range(1, groups[g]):
            scatter(c, g, j).wait_recv()
        own = pl.ds(mine[g] * lengths[g + 1], lengths[g + 1])
        total = partial[c, own] if g == 0 else sums[g - 1][c, own]
        for j in range(1, groups[g]):
            total = total + arrived[g][c, j]
        if g + 1 < stages:
            sums[g][c] = total
        else:
            full[c, pl.ds(bases[stages], lengths[stages])] = total

    def start_gather(c, g):
        for j in range(1, groups[g]):
            gather(c, g, j, mine[g]).start()

    def finish_gather(c, g):
        for j in range(1, groups[g]):
            gather(c, g, j, lax.rem(mine[g] + groups[g] - j, groups[g])).wait_recv()

    half = lax.broadcasted_iota(jnp.int32, (channels, LANES), 1) < LANES // 2
    tiles = channels // BS
    pairs = (taps + 1) // 2
    per_chunk = full.shape[1] // tiles

    for b in range(blocks):
        masked = features[b] * voxel_mask[pl.ds(b, 1), :]
        high = masked.astype(jnp.bfloat16)
        low_part = (masked - high.astype(jnp.float32)).astype(jnp.bfloat16)
        split_input[:, pl.ds(b * volume, volume)] = jnp.concatenate([high, low_part], axis=0)

    def tap_pair(n):
        span = [k for k in (2 * n, 2 * n + 1) if k < taps]
        rows = jnp.concatenate(
            [
                jnp.concatenate([window(windows, b, k, volume) for k in span], axis=1)
                for b in range(blocks)
            ],
            axis=0,
        )
        wide = jnp.dot(split_input[...], rows, preferred_element_type=jnp.float32)
        wide = wide[:channels] + wide[channels:]
        parts = [wide[:, m * LANES : (m + 1) * LANES] for m in range(len(span))]
        parts = [v + pltpu.roll(v, LANES // 2, 1) for v in parts]
        if len(parts) == 1:
            spare = jnp.zeros((channels - BS, LANES), jnp.float32)
            parts.append(
                jnp.concatenate([pltpu.roll(bias[...], LANES // 2, 1), spare], axis=0)
            )
        return jnp.where(half, *parts).reshape(tiles, BS, LANES)

    def products(c):
        for m in range(per_chunk):
            n = c * per_chunk + m
            partial[c, pl.ds(m * tiles, tiles)] = (
                tap_pair(n) if n < pairs else jnp.zeros((tiles, BS, LANES), jnp.float32)
            )

    def input_block(b):
        whole = jnp.concatenate([window(windows, b, k, volume) for k in range(taps)], axis=1)
        result = lax.dot_general(
            whole, split_weights[...], (((1,), (1,)), ((), ())), preferred_element_type=jnp.float32
        )
        result = (result + pltpu.roll(result, LANES // 2, 1)).T
        input_grad[b] = result[:channels] * voxel_mask[pl.ds(b, 1), :]

    products(0)
    pl.semaphore_wait(barrier, sum(groups) - stages)
    start_scatter(0, 0)
    for c in range(1, chunks):
        products(c)
        start_scatter(c, 0)

    def prepare_weights():
        for k in range(taps):
            value = weights[k]
            high = value.astype(jnp.bfloat16)
            low_part = (value - high.astype(jnp.float32)).astype(jnp.bfloat16)
            line = jnp.concatenate([high, low_part], axis=0)
            split_weights[:, pl.ds(k * LANES, LANES)] = jnp.concatenate([line, line], axis=1)

    queue = [prepare_weights] + [functools.partial(input_block, b) for b in range(blocks)]
    for g in range(stages):
        for c in range(chunks):
            finish_scatter(c, g)
            start_scatter(c, g + 1) if g + 1 < stages else start_gather(c, g)
        for _ in range(2):
            if queue:
                queue.pop(0)()
    for g in reversed(range(stages)):
        for c in range(chunks):
            finish_gather(c, g)
            if g:
                start_gather(c, g - 1)
        if queue:
            queue.pop(0)()
    for work in queue:
        work()

    for g in range(stages):
        for c in range(chunks):
            for j in range(1, groups[g]):
                scatter(c, g, j).wait_send()
                gather(c, g, j, mine[g]).wait_send()


def finish_kernel(scaling, full, result, input_grad, kernel_grad, bias_grad, sem):
    copy = pltpu.make_async_copy(result, input_grad, sem.at[0])
    copy.start()
    taps, channels = kernel_grad.shape[:2]
    tiles = channels // BS
    per_chunk = full.shape[1] // tiles
    for n in range((taps + 1) // 2):
        c, m = divmod(n, per_chunk)
        value = full[c, pl.ds(m * tiles, tiles)].reshape(channels, LANES) * scaling
        kernel_grad[2 * n] = value[:, :channels]
        if 2 * n + 1 < taps:
            kernel_grad[2 * n + 1] = pltpu.roll(value, LANES // 2, 1)[:, :channels]
        else:
            bias_grad[...] = pltpu.roll(value[:BS], LANES // 2, 1)[:1, :channels]
    copy.wait()


def stage_sizes(sizes):
    pair = 2 if sizes[0] % 2 == 0 else 1
    return pair, sizes[0] // pair * sizes[1], sizes[2]


def in_hbm(array):
    return pltpu.with_memory_space_constraint(array, pltpu.HBM)


def shards(sizes, features, preact, cotangent, kernel, active, owner_dir, owner_slot, send_list):
    blocks, channels, volume = features.shape
    listed = send_list.shape[0]
    taps = kernel.shape[0]
    vmem = pl.BlockSpec(memory_space=pltpu.VMEM)
    smem = pl.BlockSpec(memory_space=pltpu.SMEM)
    shaped = jax.ShapeDtypeStruct
    rows = (BS * BS // 2, BS, BS)
    sheets = [(len(g), listed, r, LANES) for g, r in zip(GROUPS, rows)]
    sheets[2] = (len(CORNERS), -(-listed // BS) * BS, LANES)
    far = pl.BlockSpec(memory_space=pltpu.HBM)
    split_grad, bias, mask, *landed = pl.pallas_call(
        functools.partial(halo_kernel, sizes),
        out_shape=[
            shaped((blocks, volume, LANES), jnp.float32),
            shaped((BS, LANES), jnp.float32),
            shaped(active.shape, jnp.float32),
        ]
        + [shaped(s, jnp.float32) for s in sheets],
        in_specs=[smem, far, far, far],
        out_specs=[vmem] * 6,
        scratch_shapes=[
            pltpu.VMEM((blocks, volume, LANES), jnp.float32),
            pltpu.VMEM((volume, LANES), jnp.float32),
        ]
        + [pltpu.VMEM(a.shape, a.dtype) for a in (preact, cotangent, active)]
        + [pltpu.VMEM(s, jnp.float32) for s in sheets]
        + [pltpu.SemaphoreType.DMA((len(HEADINGS),))] * 2
        + [pltpu.SemaphoreType.DMA((2 * blocks + 1,))],
        compiler_params=pltpu.CompilerParams(
            collective_id=0, has_side_effects=True, vmem_limit_bytes=20 * 2**20
        ),
        name="halo",
    )(*[in_hbm(a) for a in (send_list, preact, cotangent, active)])
    windows = pl.pallas_call(
        window_kernel,
        out_shape=shaped((blocks, 9, (BS + 2) * BS * BS, LANES), jnp.bfloat16),
        in_specs=[smem, smem] + [vmem] * 4,
        out_specs=vmem,
        scratch_shapes=[pltpu.VMEM(((BS + 2) * CUBE_STEPS[0], LANES), jnp.float32)],
        compiler_params=pltpu.CompilerParams(vmem_limit_bytes=20 * 2**20),
        name="windows",
    )(in_hbm(owner_dir), in_hbm(owner_slot), split_grad, *landed)
    groups, chunks = stage_sizes(sizes), 2
    pair_tiles = channels // BS
    step = chunks * math.lcm(math.prod(groups), pair_tiles)
    tiles = -(-((taps + 1) // 2 * pair_tiles) // step) * step // chunks
    lengths = [tiles]
    for n in groups:
        lengths.append(lengths[-1] // n)
    result, full = pl.pallas_call(
        functools.partial(conv_kernel, sizes, chunks),
        out_shape=[
            shaped(features.shape, jnp.float32),
            shaped((chunks, tiles, BS, LANES), jnp.float32),
        ],
        in_specs=[vmem] * 5,
        out_specs=[vmem] * 2,
        scratch_shapes=[
            pltpu.VMEM((chunks, tiles, BS, LANES), jnp.float32),
            pltpu.VMEM((2 * channels, taps * LANES), jnp.bfloat16),
            pltpu.VMEM((2 * channels, blocks * volume), jnp.bfloat16),
        ]
        + [pltpu.VMEM((chunks, n, m, BS, LANES), jnp.float32) for n, m in zip(groups, lengths[1:])]
        + [pltpu.VMEM((chunks, m, BS, LANES), jnp.float32) for m in lengths[1:]]
        + [pltpu.SemaphoreType.DMA((chunks, n)) for n in groups for _ in range(4)],
        compiler_params=pltpu.CompilerParams(
            collective_id=1, has_side_effects=True, vmem_limit_bytes=32 * 2**20
        ),
        name="conv",
    )(windows, features, mask, kernel, bias)
    scaling = (volume * blocks * lax.axis_size(AXES)) ** (-0.5)
    input_grad, kernel_grad, bias_grad = pl.pallas_call(
        functools.partial(finish_kernel, scaling),
        out_shape=[
            shaped(features.shape, jnp.float32),
            shaped(kernel.shape, jnp.float32),
            shaped((1, channels), jnp.float32),
        ],
        in_specs=[vmem, pl.BlockSpec(memory_space=pl.ANY)],
        out_specs=[pl.BlockSpec(memory_space=pl.ANY), vmem, vmem],
        scratch_shapes=[pltpu.SemaphoreType.DMA((1,))],
        compiler_params=pltpu.CompilerParams(vmem_limit_bytes=16 * 2**20),
        name="finish",
    )(full, result)
    return input_grad, kernel_grad, bias_grad.reshape(channels)


def solution(mesh):
    whole = P(AXES, None, None)
    table = P(AXES, None)
    sizes = tuple(mesh.shape[axis] for axis in AXES)
    return jax.shard_map(
        functools.partial(shards, sizes),
        mesh=mesh,
        in_specs=(whole, whole, whole, P(), table, table, table, P(AXES)),
        out_specs=(whole, P(), P()),
        check_vma=False,
    )
```

```python
import functools
import itertools
import math

import jax
import jax.numpy as jnp
from jax import lax
from jax.experimental import pallas as pl
from jax.experimental.pallas import tpu as pltpu
from jax.sharding import PartitionSpec as P

BS = 8
LANES = 128
AXES = ("gx", "gy", "gz")
MESH = pl.DeviceIdType.MESH
DEPTH = 3 * BS
CUBE_STEPS = ((BS + 2) * DEPTH, DEPTH, 1)
BLOCK_STEPS = (BS * BS, BS, 1)
HEADINGS = [m for m in itertools.product((-1, 0, 1), repeat=3) if m != (0, 0, 0)]
FACES = [m for m in HEADINGS if sum(map(abs, m)) == 1]
EDGES = [m for m in HEADINGS if sum(map(abs, m)) == 2]
CORNERS = [m for m in HEADINGS if sum(map(abs, m)) == 3]
GROUPS = (FACES, EDGES, CORNERS)


def silu_slope(preact):
    sigmoid_value = jax.nn.sigmoid(preact)
    return sigmoid_value * (1.0 + preact * (1.0 - sigmoid_value))


def place(move):
    group = sum(map(abs, move)) - 1
    return group, GROUPS[group].index(move)


def side_row(move):
    return sum(step * (BS - 1) for step, m in zip(BLOCK_STEPS, move) if m == 1)


def free_axes(move):
    return [axis for axis in range(3) if move[axis] == 0]


def split_lanes(value):
    high = value.astype(jnp.bfloat16).astype(jnp.float32)
    return high + pltpu.roll(value - high, LANES // 2, 1)


def halo_kernel(
    sizes, send_list, preact_far, cotangent_far, active_far, split_grad,
    bias, mask, face_in, edge_in, corner_in, grad, picked, preact, cotangent, active,
    face_out, edge_out, corner_out, send_sem, recv_sem, fetch_sem,
):
    blocks, channels, volume = preact.shape
    listed = send_list.shape[0]
    fetch_active = pltpu.make_async_copy(active_far, active, fetch_sem.at[2 * blocks])
    fetches = [
        [
            pltpu.make_async_copy(far.at[b], near.at[b], fetch_sem.at[2 * b + n])
            for n, (far, near) in enumerate(((preact_far, preact), (cotangent_far, cotangent)))
        ]
        for b in range(blocks)
    ]
    fetch_active.start()
    for fetch in sum(fetches, []):
        fetch.start()
    here = [lax.axis_index(axis) for axis in AXES]

    def inside(move):
        checks = []
        for axis in range(3):
            if move[axis] == 1:
                checks.append((here[axis] < sizes[axis] - 1).astype(jnp.int32))
            elif move[axis] == -1:
                checks.append((here[axis] > 0).astype(jnp.int32))
        return functools.reduce(lambda a, b: a * b, checks)

    live = {move: inside(move) for move in HEADINGS}
    target = {move: tuple(h + m for h, m in zip(here, move)) for move in HEADINGS}
    barrier = pltpu.get_barrier_semaphore()
    for move in HEADINGS:
        @pl.when(live[move] == 1)
        def _():
            pl.semaphore_signal(barrier, inc=1, device_id=target[move], device_id_type=MESH)

    total = jnp.zeros((1, LANES), jnp.float32)
    fetch_active.wait()
    mask[...] = active[...].astype(jnp.float32)
    for b in range(blocks):
        for fetch in fetches[b]:
            fetch.wait()
        value = cotangent[b] * silu_slope(preact[b]) * mask[pl.ds(b, 1), :]
        rows = jnp.concatenate([value, jnp.zeros((LANES - channels, volume), jnp.float32)], axis=0).T
        grad[b] = rows
        total = total + jnp.sum(rows, axis=0, keepdims=True)
    bias[...] = jnp.broadcast_to(total, bias.shape)

    corner_out[...] = jnp.zeros_like(corner_out)
    for s in range(listed):
        entry = send_list[s]
        keep = (entry < blocks).astype(jnp.float32)
        picked[...] = grad[jnp.minimum(entry, blocks - 1)] * keep
        for f, move in enumerate(FACES):
            first, second = free_axes(move)
            base = side_row(move)
            tiles = [
                picked[pl.ds(base + u * BLOCK_STEPS[first], BS, stride=BLOCK_STEPS[second]), :]
                for u in range(BS)
            ]
            for u in range(BS // 2):
                face_out[f, s, pl.ds(u * BS, BS), :] = tiles[u] + pltpu.roll(
                    tiles[u + BS // 2], LANES // 2, 1
                )
        for f, move in enumerate(EDGES):
            (along,) = free_axes(move)
            edge_out[f, s] = picked[pl.ds(side_row(move), BS, stride=BLOCK_STEPS[along]), :]
        for f, move in enumerate(CORNERS):
            corner_out[f, pl.ds(s, 1), :] = picked[pl.ds(side_row(move), 1), :]

    count = functools.reduce(lambda a, b: a + b, [live[move] for move in HEADINGS])
    pl.semaphore_wait(barrier, count)

    sent, landed = (face_out, edge_out, corner_out), (face_in, edge_in, corner_in)

    def copy_of(move):
        group, f = place(move)
        n = HEADINGS.index(move)
        return pltpu.make_async_remote_copy(
            src_ref=sent[group].at[f],
            dst_ref=landed[group].at[f],
            send_sem=send_sem.at[n],
            recv_sem=recv_sem.at[n],
            device_id=target[move],
            device_id_type=MESH,
        )

    for move in FACES + EDGES + CORNERS:
        @pl.when(live[move] == 1)
        def _():
            copy_of(move).start()

    for b in range(blocks):
        split_grad[b] = split_lanes(grad[b])

    for move in FACES + EDGES + CORNERS:
        back = tuple(-m for m in move)

        @pl.when(live[move] == 1)
        def _():
            copy_of(move).wait_send()

        @pl.when(live[back] == 1)
        def _():
            copy_of(move).wait_recv()


def window_kernel(
    owner_dir, owner_slot, split_grad, face_in, edge_in, corner_in, windows, cube
):
    blocks = split_grad.shape[0]
    low_half = lax.broadcasted_iota(jnp.int32, (BS, LANES), 1) < LANES // 2

    def cube_row(move):
        origin = CUBE_STEPS[0] + CUBE_STEPS[1] + BS
        return origin + sum(
            step * (BS if m == 1 else -1) for step, m in zip(CUBE_STEPS, move) if m != 0
        )

    def fill_own(offset, slot):
        back = tuple(-m for m in offset)
        source, into = side_row(back), cube_row(offset)
        free = free_axes(offset)
        if not free:
            cube[pl.ds(into, 1), :] = split_grad[slot, pl.ds(source, 1), :]
            return
        along = free[-1]
        for lead in itertools.product(range(BS), repeat=len(free) - 1):
            shift = sum(BLOCK_STEPS[a] * u for a, u in zip(free, lead))
            move = sum(CUBE_STEPS[a] * u for a, u in zip(free, lead))
            cube[pl.ds(into + move, BS, stride=CUBE_STEPS[along]), :] = split_grad[
                slot, pl.ds(source + shift, BS, stride=BLOCK_STEPS[along]), :
            ]

    def fill_remote(offset, owner, slot):
        group, f = place(tuple(-m for m in owner))
        into = cube_row(offset)
        picks = [BS - 1 if offset[a] == -1 else 0 for a in range(3)]
        if group == 2:
            value = jnp.where(low_half[:1], corner_in[f, pl.ds(slot, 1), :], 0.0)
            cube[pl.ds(into, 1), :] = split_lanes(value)
        elif group == 1:
            (along,) = free_axes(owner)
            value = split_lanes(jnp.where(low_half, edge_in[f, slot], 0.0))
            if offset[along] == 0:
                cube[pl.ds(into, BS, stride=CUBE_STEPS[along]), :] = value
            else:
                at = picks[along]
                cube[pl.ds(into, 1), :] = value[at : at + 1]
        else:
            first, second = free_axes(owner)
            for u in range(BS) if offset[first] == 0 else (picks[first],):
                half, row = divmod(u, BS // 2)
                value = face_in[f, slot, pl.ds(row * BS, BS), :]
                if half:
                    value = pltpu.roll(value, LANES // 2, 1)
                value = split_lanes(jnp.where(low_half, value, 0.0))
                at_u = into + (u * CUBE_STEPS[first] if offset[first] == 0 else 0)
                if offset[second] == 0:
                    cube[pl.ds(at_u, BS, stride=CUBE_STEPS[second]), :] = value
                else:
                    at = picks[second]
                    cube[pl.ds(at_u, 1), :] = value[at : at + 1]

    def visit_block(b, carry):
        cube[...] = jnp.zeros_like(cube)
        for x in range(BS):
            for y in range(BS):
                cube[pl.ds(cube_row((0, 0, 0)) + x * CUBE_STEPS[0] + y * CUBE_STEPS[1], BS), :] = (
                    split_grad[b, pl.ds((x * BS + y) * BS, BS), :]
                )
        for offset in HEADINGS:
            o = 9 * (offset[0] + 1) + 3 * (offset[1] + 1) + offset[2] + 1
            code, slot = owner_dir[b, o], owner_slot[b, o]

            @pl.when(code != 27)
            def _():
                @pl.when(code == 13)
                def _():
                    fill_own(offset, slot)

                for owner in itertools.product(*[(0,) if m == 0 else (0, m) for m in offset]):
                    if owner != (0, 0, 0):
                        @pl.when(code == 9 * (owner[0] + 1) + 3 * (owner[1] + 1) + owner[2] + 1)
                        def _():
                            fill_remote(offset, owner, slot)

        for ky in (-1, 0, 1):
            for kz in (-1, 0, 1):
                for x in range(BS + 2):
                    tiles = [
                        cube[pl.ds(x * CUBE_STEPS[0] + (y + 1 - ky) * CUBE_STEPS[1] + BS - kz, BS), :]
                        for y in range(BS)
                    ]
                    windows[b, 3 * (ky + 1) + kz + 1, pl.ds(x * BS * BS, BS * BS), :] = (
                        jnp.concatenate(tiles, axis=0).astype(jnp.bfloat16)
                    )
        return carry

    lax.fori_loop(0, blocks, visit_block, 0)


def window(windows, b, k, volume):
    kx, q = divmod(k, 9)
    return windows[b, q, pl.ds((2 - kx) * BS * BS, volume), :]


def conv_kernel(
    sizes, chunks, windows, features, voxel_mask, weights, bias, input_grad, full,
    partial, split_weights, split_input, *rest,
):
    blocks, channels, volume = features.shape
    taps = weights.shape[0]
    here = [lax.axis_index(axis) for axis in AXES]
    groups = stage_sizes(sizes)
    stages = len(groups)
    arrived, sums, sems = rest[:stages], rest[stages : 2 * stages], rest[2 * stages :]
    pair = groups[0]
    column, low = here[0] // pair, lax.rem(here[0], pair)
    mine = (low, column * sizes[1] + here[1], here[2])

    def member(g, j):
        p = lax.rem(mine[g] + j, groups[g])
        if g == 0:
            return p, (column * pair + p, here[1], here[2])
        if g == 1:
            return p, (p // sizes[1] * pair + low, lax.rem(p, sizes[1]), here[2])
        return p, (here[0], here[1], p)

    lengths = [full.shape[1]]
    for n in groups:
        lengths.append(lengths[-1] // n)
    bases = [0]
    for g in range(stages):
        bases.append(bases[-1] + mine[g] * lengths[g + 1])

    barrier = pltpu.get_barrier_semaphore()
    for g, n in enumerate(groups):
        for j in range(1, n):
            pl.semaphore_signal(barrier, inc=1, device_id=member(g, j)[1], device_id_type=MESH)

    def scatter(c, g, j):
        p, device = member(g, j)
        source = partial.at[c] if g == 0 else sums[g - 1].at[c]
        return pltpu.make_async_remote_copy(
            src_ref=source.at[pl.ds(p * lengths[g + 1], lengths[g + 1])],
            dst_ref=arrived[g].at[c, j],
            send_sem=sems[4 * g].at[c, j],
            recv_sem=sems[4 * g + 1].at[c, j],
            device_id=device,
            device_id_type=MESH,
        )

    def gather(c, g, j, place_of):
        area = full.at[c, pl.ds(bases[g] + place_of * lengths[g + 1], lengths[g + 1])]
        return pltpu.make_async_remote_copy(
            src_ref=area,
            dst_ref=area,
            send_sem=sems[4 * g + 2].at[c, j],
            recv_sem=sems[4 * g + 3].at[c, j],
            device_id=member(g, j)[1],
            device_id_type=MESH,
        )

    def start_scatter(c, g):
        for j in range(1, groups[g]):
            scatter(c, g, j).start()

    def finish_scatter(c, g):
        for j in range(1, groups[g]):
            scatter(c, g, j).wait_recv()
        own = pl.ds(mine[g] * lengths[g + 1], lengths[g + 1])
        total = partial[c, own] if g == 0 else sums[g - 1][c, own]
        for j in range(1, groups[g]):
            total = total + arrived[g][c, j]
        if g + 1 < stages:
            sums[g][c] = total
        else:
            full[c, pl.ds(bases[stages], lengths[stages])] = total

    def start_gather(c, g):
        for j in range(1, groups[g]):
            gather(c, g, j, mine[g]).start()

    def finish_gather(c, g):
        for j in range(1, groups[g]):
            gather(c, g, j, lax.rem(mine[g] + groups[g] - j, groups[g])).wait_recv()

    half = lax.broadcasted_iota(jnp.int32, (channels, LANES), 1) < LANES // 2
    tiles = channels // BS
    pairs = (taps + 1) // 2
    per_chunk = full.shape[1] // tiles

    for b in range(blocks):
        masked = features[b] * voxel_mask[pl.ds(b, 1), :]
        high = masked.astype(jnp.bfloat16)
        low_part = (masked - high.astype(jnp.float32)).astype(jnp.bfloat16)
        split_input[:, pl.ds(b * volume, volume)] = jnp.concatenate([high, low_part], axis=0)

    def tap_pair(n):
        span = [k for k in (2 * n, 2 * n + 1) if k < taps]
        rows = jnp.concatenate(
            [
                jnp.concatenate([window(windows, b, k, volume) for k in span], axis=1)
                for b in range(blocks)
            ],
            axis=0,
        )
        wide = jnp.dot(split_input[...], rows, preferred_element_type=jnp.float32)
        wide = wide[:channels] + wide[channels:]
        parts = [wide[:, m * LANES : (m + 1) * LANES] for m in range(len(span))]
        parts = [v + pltpu.roll(v, LANES // 2, 1) for v in parts]
        if len(parts) == 1:
            spare = jnp.zeros((channels - BS, LANES), jnp.float32)
            parts.append(
                jnp.concatenate([pltpu.roll(bias[...], LANES // 2, 1), spare], axis=0)
            )
        return jnp.where(half, *parts).reshape(tiles, BS, LANES)

    def products(c):
        for m in range(per_chunk):
            n = c * per_chunk + m
            partial[c, pl.ds(m * tiles, tiles)] = (
                tap_pair(n) if n < pairs else jnp.zeros((tiles, BS, LANES), jnp.float32)
            )

    def input_block(b):
        whole = jnp.concatenate([window(windows, b, k, volume) for k in range(taps)], axis=1)
        result = lax.dot_general(
            whole, split_weights[...], (((1,), (1,)), ((), ())), preferred_element_type=jnp.float32
        )
        result = (result + pltpu.roll(result, LANES // 2, 1)).T
        input_grad[b] = result[:channels] * voxel_mask[pl.ds(b, 1), :]

    def advance(c, step):
        if step < stages:
            finish_scatter(c, step)
            start_scatter(c, step + 1) if step + 1 < stages else start_gather(c, step)
        else:
            g = 2 * stages - 1 - step
            finish_gather(c, g)
            if g:
                start_gather(c, g - 1)

    def prepare_weights():
        for k in range(taps):
            value = weights[k]
            high = value.astype(jnp.bfloat16)
            low_part = (value - high.astype(jnp.float32)).astype(jnp.bfloat16)
            line = jnp.concatenate([high, low_part], axis=0)
            split_weights[:, pl.ds(k * LANES, LANES)] = jnp.concatenate([line, line], axis=1)

    queue = [prepare_weights] + [functools.partial(input_block, b) for b in range(blocks)]
    for step in range(chunks + 2 * stages):
        if step < chunks:
            products(step)
            if step == 0:
                pl.semaphore_wait(barrier, sum(groups) - stages)
            start_scatter(step, 0)
        elif queue:
            queue.pop(0)()
        for c in range(chunks):
            if 0 <= step - 1 - c < 2 * stages:
                advance(c, step - 1 - c)
    for work in queue:
        work()

    for g in range(stages):
        for c in range(chunks):
            for j in range(1, groups[g]):
                scatter(c, g, j).wait_send()
                gather(c, g, j, mine[g]).wait_send()


def finish_kernel(scaling, full, result, input_grad, kernel_grad, bias_grad, sem):
    copy = pltpu.make_async_copy(result, input_grad, sem.at[0])
    copy.start()
    taps, channels = kernel_grad.shape[:2]
    tiles = channels // BS
    per_chunk = full.shape[1] // tiles
    for n in range((taps + 1) // 2):
        c, m = divmod(n, per_chunk)
        value = full[c, pl.ds(m * tiles, tiles)].reshape(channels, LANES) * scaling
        kernel_grad[2 * n] = value[:, :channels]
        if 2 * n + 1 < taps:
            kernel_grad[2 * n + 1] = pltpu.roll(value, LANES // 2, 1)[:, :channels]
        else:
            bias_grad[...] = pltpu.roll(value[:BS], LANES // 2, 1)[:1, :channels]
    copy.wait()


def stage_sizes(sizes):
    pair = 2 if sizes[0] % 2 == 0 else 1
    return pair, sizes[0] // pair * sizes[1], sizes[2]


def in_hbm(array):
    return pltpu.with_memory_space_constraint(array, pltpu.HBM)


def shards(sizes, features, preact, cotangent, kernel, active, owner_dir, owner_slot, send_list):
    blocks, channels, volume = features.shape
    listed = send_list.shape[0]
    taps = kernel.shape[0]
    vmem = pl.BlockSpec(memory_space=pltpu.VMEM)
    smem = pl.BlockSpec(memory_space=pltpu.SMEM)
    shaped = jax.ShapeDtypeStruct
    rows = (BS * BS // 2, BS, BS)
    sheets = [(len(g), listed, r, LANES) for g, r in zip(GROUPS, rows)]
    sheets[2] = (len(CORNERS), -(-listed // BS) * BS, LANES)
    far = pl.BlockSpec(memory_space=pltpu.HBM)
    split_grad, bias, mask, *landed = pl.pallas_call(
        functools.partial(halo_kernel, sizes),
        out_shape=[
            shaped((blocks, volume, LANES), jnp.float32),
            shaped((BS, LANES), jnp.float32),
            shaped(active.shape, jnp.float32),
        ]
        + [shaped(s, jnp.float32) for s in sheets],
        in_specs=[smem, far, far, far],
        out_specs=[vmem] * 6,
        scratch_shapes=[
            pltpu.VMEM((blocks, volume, LANES), jnp.float32),
            pltpu.VMEM((volume, LANES), jnp.float32),
        ]
        + [pltpu.VMEM(a.shape, a.dtype) for a in (preact, cotangent, active)]
        + [pltpu.VMEM(s, jnp.float32) for s in sheets]
        + [pltpu.SemaphoreType.DMA((len(HEADINGS),))] * 2
        + [pltpu.SemaphoreType.DMA((2 * blocks + 1,))],
        compiler_params=pltpu.CompilerParams(
            collective_id=0, has_side_effects=True, vmem_limit_bytes=20 * 2**20
        ),
        name="halo",
    )(*[in_hbm(a) for a in (send_list, preact, cotangent, active)])
    windows = pl.pallas_call(
        window_kernel,
        out_shape=shaped((blocks, 9, (BS + 2) * BS * BS, LANES), jnp.bfloat16),
        in_specs=[smem, smem] + [vmem] * 4,
        out_specs=vmem,
        scratch_shapes=[pltpu.VMEM(((BS + 2) * CUBE_STEPS[0], LANES), jnp.float32)],
        compiler_params=pltpu.CompilerParams(vmem_limit_bytes=20 * 2**20),
        name="windows",
    )(in_hbm(owner_dir), in_hbm(owner_slot), split_grad, *landed)
    groups = stage_sizes(sizes)
    chunks = min(4, max(1, 2 * channels // math.prod(groups)))
    pair_tiles = channels // BS
    step = chunks * math.lcm(math.prod(groups), pair_tiles)
    tiles = -(-((taps + 1) // 2 * pair_tiles) // step) * step // chunks
    lengths = [tiles]
    for n in groups:
        lengths.append(lengths[-1] // n)
    result, full = pl.pallas_call(
        functools.partial(conv_kernel, sizes, chunks),
        out_shape=[
            shaped(features.shape, jnp.float32),
            shaped((chunks, tiles, BS, LANES), jnp.float32),
        ],
        in_specs=[vmem] * 5,
        out_specs=[vmem] * 2,
        scratch_shapes=[
            pltpu.VMEM((chunks, tiles, BS, LANES), jnp.float32),
            pltpu.VMEM((2 * channels, taps * LANES), jnp.bfloat16),
            pltpu.VMEM((2 * channels, blocks * volume), jnp.bfloat16),
        ]
        + [pltpu.VMEM((chunks, n, m, BS, LANES), jnp.float32) for n, m in zip(groups, lengths[1:])]
        + [pltpu.VMEM((chunks, m, BS, LANES), jnp.float32) for m in lengths[1:]]
        + [pltpu.SemaphoreType.DMA((chunks, n)) for n in groups for _ in range(4)],
        compiler_params=pltpu.CompilerParams(
            collective_id=1, has_side_effects=True, vmem_limit_bytes=32 * 2**20
        ),
        name="conv",
    )(windows, features, mask, kernel, bias)
    scaling = (volume * blocks * lax.axis_size(AXES)) ** (-0.5)
    input_grad, kernel_grad, bias_grad = pl.pallas_call(
        functools.partial(finish_kernel, scaling),
        out_shape=[
            shaped(features.shape, jnp.float32),
            shaped(kernel.shape, jnp.float32),
            shaped((1, channels), jnp.float32),
        ],
        in_specs=[vmem, pl.BlockSpec(memory_space=pl.ANY)],
        out_specs=[pl.BlockSpec(memory_space=pl.ANY), vmem, vmem],
        scratch_shapes=[pltpu.SemaphoreType.DMA((1,))],
        compiler_params=pltpu.CompilerParams(vmem_limit_bytes=16 * 2**20),
        name="finish",
    )(full, result)
    return input_grad, kernel_grad, bias_grad.reshape(channels)


def solution(mesh):
    whole = P(AXES, None, None)
    table = P(AXES, None)
    sizes = tuple(mesh.shape[axis] for axis in AXES)
    return jax.shard_map(
        functools.partial(shards, sizes),
        mesh=mesh,
        in_specs=(whole, whole, whole, P(), table, table, table, P(AXES)),
        out_specs=(whole, P(), P()),
        check_vma=False,
    )
```

```python
import functools
import itertools
import math

import jax
import jax.numpy as jnp
from jax import lax
from jax.experimental import pallas as pl
from jax.experimental.pallas import tpu as pltpu
from jax.sharding import PartitionSpec as P

BS = 8
LANES = 128
AXES = ("gx", "gy", "gz")
MESH = pl.DeviceIdType.MESH
DEPTH = 3 * BS
CUBE_STEPS = ((BS + 2) * DEPTH, DEPTH, 1)
BLOCK_STEPS = (BS * BS, BS, 1)
HEADINGS = [m for m in itertools.product((-1, 0, 1), repeat=3) if m != (0, 0, 0)]
FACES = [m for m in HEADINGS if sum(map(abs, m)) == 1]
EDGES = [m for m in HEADINGS if sum(map(abs, m)) == 2]
CORNERS = [m for m in HEADINGS if sum(map(abs, m)) == 3]
GROUPS = (FACES, EDGES, CORNERS)


def silu_slope(preact):
    sigmoid_value = jax.nn.sigmoid(preact)
    return sigmoid_value * (1.0 + preact * (1.0 - sigmoid_value))


def place(move):
    group = sum(map(abs, move)) - 1
    return group, GROUPS[group].index(move)


def side_row(move):
    return sum(step * (BS - 1) for step, m in zip(BLOCK_STEPS, move) if m == 1)


def free_axes(move):
    return [axis for axis in range(3) if move[axis] == 0]


def split_lanes(value):
    high = value.astype(jnp.bfloat16).astype(jnp.float32)
    return high + pltpu.roll(value - high, LANES // 2, 1)


def halo_kernel(
    sizes, send_list, preact_far, cotangent_far, active_far, split_grad,
    bias, mask, face_in, edge_in, corner_in, grad, picked, preact, cotangent, active,
    face_out, edge_out, corner_out, send_sem, recv_sem, fetch_sem,
):
    blocks, channels, volume = preact.shape
    listed = send_list.shape[0]
    fetch_active = pltpu.make_async_copy(active_far, active, fetch_sem.at[2 * blocks])
    fetches = [
        [
            pltpu.make_async_copy(far.at[b], near.at[b], fetch_sem.at[2 * b + n])
            for n, (far, near) in enumerate(((preact_far, preact), (cotangent_far, cotangent)))
        ]
        for b in range(blocks)
    ]
    fetch_active.start()
    for fetch in sum(fetches, []):
        fetch.start()
    here = [lax.axis_index(axis) for axis in AXES]

    def inside(move):
        checks = []
        for axis in range(3):
            if move[axis] == 1:
                checks.append((here[axis] < sizes[axis] - 1).astype(jnp.int32))
            elif move[axis] == -1:
                checks.append((here[axis] > 0).astype(jnp.int32))
        return functools.reduce(lambda a, b: a * b, checks)

    live = {move: inside(move) for move in HEADINGS}
    target = {move: tuple(h + m for h, m in zip(here, move)) for move in HEADINGS}
    barrier = pltpu.get_barrier_semaphore()
    for move in HEADINGS:
        @pl.when(live[move] == 1)
        def _():
            pl.semaphore_signal(barrier, inc=1, device_id=target[move], device_id_type=MESH)

    total = jnp.zeros((1, LANES), jnp.float32)
    fetch_active.wait()
    mask[...] = active[...].astype(jnp.float32)
    for b in range(blocks):
        for fetch in fetches[b]:
            fetch.wait()
        value = cotangent[b] * silu_slope(preact[b]) * mask[pl.ds(b, 1), :]
        rows = jnp.concatenate([value, jnp.zeros((LANES - channels, volume), jnp.float32)], axis=0).T
        grad[b] = rows
        total = total + jnp.sum(rows, axis=0, keepdims=True)
    bias[...] = jnp.broadcast_to(total, bias.shape)

    corner_out[...] = jnp.zeros_like(corner_out)
    for s in range(listed):
        entry = send_list[s]
        keep = (entry < blocks).astype(jnp.float32)
        picked[...] = grad[jnp.minimum(entry, blocks - 1)] * keep
        for f, move in enumerate(FACES):
            first, second = free_axes(move)
            base = side_row(move)
            tiles = [
                picked[pl.ds(base + u * BLOCK_STEPS[first], BS, stride=BLOCK_STEPS[second]), :]
                for u in range(BS)
            ]
            for u in range(BS // 2):
                face_out[f, s, pl.ds(u * BS, BS), :] = tiles[u] + pltpu.roll(
                    tiles[u + BS // 2], LANES // 2, 1
                )
        for f, move in enumerate(EDGES):
            (along,) = free_axes(move)
            edge_out[f, s] = picked[pl.ds(side_row(move), BS, stride=BLOCK_STEPS[along]), :]
        for f, move in enumerate(CORNERS):
            corner_out[f, pl.ds(s, 1), :] = picked[pl.ds(side_row(move), 1), :]

    count = functools.reduce(lambda a, b: a + b, [live[move] for move in HEADINGS])
    pl.semaphore_wait(barrier, count)

    sent, landed = (face_out, edge_out, corner_out), (face_in, edge_in, corner_in)

    def copy_of(move):
        group, f = place(move)
        n = HEADINGS.index(move)
        return pltpu.make_async_remote_copy(
            src_ref=sent[group].at[f],
            dst_ref=landed[group].at[f],
            send_sem=send_sem.at[n],
            recv_sem=recv_sem.at[n],
            device_id=target[move],
            device_id_type=MESH,
        )

    for move in FACES + EDGES + CORNERS:
        @pl.when(live[move] == 1)
        def _():
            copy_of(move).start()

    for b in range(blocks):
        split_grad[b] = split_lanes(grad[b])

    for move in FACES + EDGES + CORNERS:
        back = tuple(-m for m in move)

        @pl.when(live[move] == 1)
        def _():
            copy_of(move).wait_send()

        @pl.when(live[back] == 1)
        def _():
            copy_of(move).wait_recv()


def window_kernel(
    owner_dir, owner_slot, split_grad, face_in, edge_in, corner_in, windows, cube
):
    blocks = split_grad.shape[0]
    low_half = lax.broadcasted_iota(jnp.int32, (BS, LANES), 1) < LANES // 2

    def cube_row(move):
        origin = CUBE_STEPS[0] + CUBE_STEPS[1] + BS
        return origin + sum(
            step * (BS if m == 1 else -1) for step, m in zip(CUBE_STEPS, move) if m != 0
        )

    def fill_own(offset, slot):
        back = tuple(-m for m in offset)
        source, into = side_row(back), cube_row(offset)
        free = free_axes(offset)
        if not free:
            cube[pl.ds(into, 1), :] = split_grad[slot, pl.ds(source, 1), :]
            return
        along = free[-1]
        for lead in itertools.product(range(BS), repeat=len(free) - 1):
            shift = sum(BLOCK_STEPS[a] * u for a, u in zip(free, lead))
            move = sum(CUBE_STEPS[a] * u for a, u in zip(free, lead))
            cube[pl.ds(into + move, BS, stride=CUBE_STEPS[along]), :] = split_grad[
                slot, pl.ds(source + shift, BS, stride=BLOCK_STEPS[along]), :
            ]

    def fill_remote(offset, owner, slot):
        group, f = place(tuple(-m for m in owner))
        into = cube_row(offset)
        picks = [BS - 1 if offset[a] == -1 else 0 for a in range(3)]
        if group == 2:
            value = jnp.where(low_half[:1], corner_in[f, pl.ds(slot, 1), :], 0.0)
            cube[pl.ds(into, 1), :] = split_lanes(value)
        elif group == 1:
            (along,) = free_axes(owner)
            value = split_lanes(jnp.where(low_half, edge_in[f, slot], 0.0))
            if offset[along] == 0:
                cube[pl.ds(into, BS, stride=CUBE_STEPS[along]), :] = value
            else:
                at = picks[along]
                cube[pl.ds(into, 1), :] = value[at : at + 1]
        else:
            first, second = free_axes(owner)
            for u in range(BS) if offset[first] == 0 else (picks[first],):
                half, row = divmod(u, BS // 2)
                value = face_in[f, slot, pl.ds(row * BS, BS), :]
                if half:
                    value = pltpu.roll(value, LANES // 2, 1)
                value = split_lanes(jnp.where(low_half, value, 0.0))
                at_u = into + (u * CUBE_STEPS[first] if offset[first] == 0 else 0)
                if offset[second] == 0:
                    cube[pl.ds(at_u, BS, stride=CUBE_STEPS[second]), :] = value
                else:
                    at = picks[second]
                    cube[pl.ds(at_u, 1), :] = value[at : at + 1]

    def visit_block(b, carry):
        cube[...] = jnp.zeros_like(cube)
        for x in range(BS):
            for y in range(BS):
                cube[pl.ds(cube_row((0, 0, 0)) + x * CUBE_STEPS[0] + y * CUBE_STEPS[1], BS), :] = (
                    split_grad[b, pl.ds((x * BS + y) * BS, BS), :]
                )
        for offset in HEADINGS:
            o = 9 * (offset[0] + 1) + 3 * (offset[1] + 1) + offset[2] + 1
            code, slot = owner_dir[b, o], owner_slot[b, o]

            @pl.when(code != 27)
            def _():
                @pl.when(code == 13)
                def _():
                    fill_own(offset, slot)

                for owner in itertools.product(*[(0,) if m == 0 else (0, m) for m in offset]):
                    if owner != (0, 0, 0):
                        @pl.when(code == 9 * (owner[0] + 1) + 3 * (owner[1] + 1) + owner[2] + 1)
                        def _():
                            fill_remote(offset, owner, slot)

        for ky in (-1, 0, 1):
            for kz in (-1, 0, 1):
                for x in range(BS + 2):
                    tiles = [
                        cube[pl.ds(x * CUBE_STEPS[0] + (y + 1 - ky) * CUBE_STEPS[1] + BS - kz, BS), :]
                        for y in range(BS)
                    ]
                    windows[b, 3 * (ky + 1) + kz + 1, pl.ds(x * BS * BS, BS * BS), :] = (
                        jnp.concatenate(tiles, axis=0).astype(jnp.bfloat16)
                    )
        return carry

    lax.fori_loop(0, blocks, visit_block, 0)


def window(windows, b, k, volume):
    kx, q = divmod(k, 9)
    return windows[b, q, pl.ds((2 - kx) * BS * BS, volume), :]


def conv_kernel(
    sizes, chunks, windows, features, voxel_mask, weights, bias, input_grad, full,
    partial, split_weights, split_input, *rest,
):
    blocks, channels, volume = features.shape
    taps = weights.shape[0]
    here = [lax.axis_index(axis) for axis in AXES]
    groups = stage_sizes(sizes)
    stages = len(groups)
    arrived, sums, sems = rest[:stages], rest[stages : 2 * stages], rest[2 * stages :]
    pair = groups[0]
    column, low = here[0] // pair, lax.rem(here[0], pair)
    mine = (low, column * sizes[1] + here[1], here[2])

    def member(g, j):
        p = lax.rem(mine[g] + j, groups[g])
        if g == 0:
            return p, (column * pair + p, here[1], here[2])
        if g == 1:
            return p, (p // sizes[1] * pair + low, lax.rem(p, sizes[1]), here[2])
        return p, (here[0], here[1], p)

    lengths = [full.shape[1]]
    for n in groups:
        lengths.append(lengths[-1] // n)
    bases = [0]
    for g in range(stages):
        bases.append(bases[-1] + mine[g] * lengths[g + 1])

    barrier = pltpu.get_barrier_semaphore()
    for g, n in enumerate(groups):
        for j in range(1, n):
            pl.semaphore_signal(barrier, inc=1, device_id=member(g, j)[1], device_id_type=MESH)

    def scatter(c, g, j):
        p, device = member(g, j)
        source = partial.at[c] if g == 0 else sums[g - 1].at[c]
        return pltpu.make_async_remote_copy(
            src_ref=source.at[pl.ds(p * lengths[g + 1], lengths[g + 1])],
            dst_ref=arrived[g].at[c, j],
            send_sem=sems[4 * g].at[c, j],
            recv_sem=sems[4 * g + 1].at[c, j],
            device_id=device,
            device_id_type=MESH,
        )

    def gather(c, g, j, place_of):
        area = full.at[c, pl.ds(bases[g] + place_of * lengths[g + 1], lengths[g + 1])]
        return pltpu.make_async_remote_copy(
            src_ref=area,
            dst_ref=area,
            send_sem=sems[4 * g + 2].at[c, j],
            recv_sem=sems[4 * g + 3].at[c, j],
            device_id=member(g, j)[1],
            device_id_type=MESH,
        )

    def start_scatter(c, g):
        for j in range(1, groups[g]):
            scatter(c, g, j).start()

    def finish_scatter(c, g):
        for j in range(1, groups[g]):
            scatter(c, g, j).wait_recv()
        own = pl.ds(mine[g] * lengths[g + 1], lengths[g + 1])
        total = partial[c, own] if g == 0 else sums[g - 1][c, own]
        for j in range(1, groups[g]):
            total = total + arrived[g][c, j]
        if g + 1 < stages:
            sums[g][c] = total
        else:
            full[c, pl.ds(bases[stages], lengths[stages])] = total

    def start_gather(c, g):
        for j in range(1, groups[g]):
            gather(c, g, j, mine[g]).start()

    def finish_gather(c, g):
        for j in range(1, groups[g]):
            gather(c, g, j, lax.rem(mine[g] + groups[g] - j, groups[g])).wait_recv()

    half = lax.broadcasted_iota(jnp.int32, (channels, LANES), 1) < LANES // 2
    tiles = channels // BS
    pairs = (taps + 1) // 2
    per_chunk = full.shape[1] // tiles

    for b in range(blocks):
        masked = features[b] * voxel_mask[pl.ds(b, 1), :]
        high = masked.astype(jnp.bfloat16)
        low_part = (masked - high.astype(jnp.float32)).astype(jnp.bfloat16)
        split_input[:, pl.ds(b * volume, volume)] = jnp.concatenate([high, low_part], axis=0)

    def tap_pair(n):
        span = [k for k in (2 * n, 2 * n + 1) if k < taps]
        rows = jnp.concatenate(
            [
                jnp.concatenate([window(windows, b, k, volume) for k in span], axis=1)
                for b in range(blocks)
            ],
            axis=0,
        )
        wide = jnp.dot(split_input[...], rows, preferred_element_type=jnp.float32)
        wide = wide[:channels] + wide[channels:]
        parts = [wide[:, m * LANES : (m + 1) * LANES] for m in range(len(span))]
        parts = [v + pltpu.roll(v, LANES // 2, 1) for v in parts]
        if len(parts) == 1:
            spare = jnp.zeros((channels - BS, LANES), jnp.float32)
            parts.append(
                jnp.concatenate([pltpu.roll(bias[...], LANES // 2, 1), spare], axis=0)
            )
        return jnp.where(half, *parts).reshape(tiles, BS, LANES)

    def products(c):
        for m in range(per_chunk):
            n = c * per_chunk + m
            partial[c, pl.ds(m * tiles, tiles)] = (
                tap_pair(n) if n < pairs else jnp.zeros((tiles, BS, LANES), jnp.float32)
            )

    def input_block(b):
        whole = jnp.concatenate([window(windows, b, k, volume) for k in range(taps)], axis=1)
        result = lax.dot_general(
            whole, split_weights[...], (((1,), (1,)), ((), ())), preferred_element_type=jnp.float32
        )
        result = (result + pltpu.roll(result, LANES // 2, 1)).T
        input_grad[b] = result[:channels] * voxel_mask[pl.ds(b, 1), :]

    def advance(c, step):
        if step < stages:
            finish_scatter(c, step)
            start_scatter(c, step + 1) if step + 1 < stages else start_gather(c, step)
        else:
            g = 2 * stages - 1 - step
            finish_gather(c, g)
            if g:
                start_gather(c, g - 1)

    def prepare_weights():
        for k in range(taps):
            value = weights[k]
            high = value.astype(jnp.bfloat16)
            low_part = (value - high.astype(jnp.float32)).astype(jnp.bfloat16)
            line = jnp.concatenate([high, low_part], axis=0)
            split_weights[:, pl.ds(k * LANES, LANES)] = jnp.concatenate([line, line], axis=1)

    queue = [prepare_weights] + [functools.partial(input_block, b) for b in range(blocks)]
    for step in range(chunks + 2 * stages):
        if step < chunks:
            products(step)
            if step == 0:
                pl.semaphore_wait(barrier, sum(groups) - stages)
            start_scatter(step, 0)
        elif queue:
            queue.pop(0)()
        for c in range(chunks):
            if 0 <= step - 1 - c < 2 * stages:
                advance(c, step - 1 - c)
    for work in queue:
        work()

    for g in range(stages):
        for c in range(chunks):
            for j in range(1, groups[g]):
                scatter(c, g, j).wait_send()
                gather(c, g, j, mine[g]).wait_send()


def finish_kernel(scaling, full, result, input_grad, kernel_grad, bias_grad, sem):
    copy = pltpu.make_async_copy(result, input_grad, sem.at[0])
    copy.start()
    taps, channels = kernel_grad.shape[:2]
    tiles = channels // BS
    per_chunk = full.shape[1] // tiles
    for n in range((taps + 1) // 2):
        c, m = divmod(n, per_chunk)
        value = full[c, pl.ds(m * tiles, tiles)].reshape(channels, LANES) * scaling
        kernel_grad[2 * n] = value[:, :channels]
        if 2 * n + 1 < taps:
            kernel_grad[2 * n + 1] = pltpu.roll(value, LANES // 2, 1)[:, :channels]
        else:
            bias_grad[...] = pltpu.roll(value[:BS], LANES // 2, 1)[:1, :channels]
    copy.wait()


def stage_sizes(sizes):
    pair = 2 if sizes[0] % 2 == 0 else 1
    return pair, sizes[0] // pair * sizes[1], sizes[2]


def in_hbm(array):
    return pltpu.with_memory_space_constraint(array, pltpu.HBM)


def shards(sizes, features, preact, cotangent, kernel, active, owner_dir, owner_slot, send_list):
    blocks, channels, volume = features.shape
    listed = send_list.shape[0]
    taps = kernel.shape[0]
    vmem = pl.BlockSpec(memory_space=pltpu.VMEM)
    smem = pl.BlockSpec(memory_space=pltpu.SMEM)
    shaped = jax.ShapeDtypeStruct
    rows = (BS * BS // 2, BS, BS)
    sheets = [(len(g), listed, r, LANES) for g, r in zip(GROUPS, rows)]
    sheets[2] = (len(CORNERS), -(-listed // BS) * BS, LANES)
    far = pl.BlockSpec(memory_space=pltpu.HBM)
    split_grad, bias, mask, *landed = pl.pallas_call(
        functools.partial(halo_kernel, sizes),
        out_shape=[
            shaped((blocks, volume, LANES), jnp.float32),
            shaped((BS, LANES), jnp.float32),
            shaped(active.shape, jnp.float32),
        ]
        + [shaped(s, jnp.float32) for s in sheets],
        in_specs=[smem, far, far, far],
        out_specs=[vmem] * 6,
        scratch_shapes=[
            pltpu.VMEM((blocks, volume, LANES), jnp.float32),
            pltpu.VMEM((volume, LANES), jnp.float32),
        ]
        + [pltpu.VMEM(a.shape, a.dtype) for a in (preact, cotangent, active)]
        + [pltpu.VMEM(s, jnp.float32) for s in sheets]
        + [pltpu.SemaphoreType.DMA((len(HEADINGS),))] * 2
        + [pltpu.SemaphoreType.DMA((2 * blocks + 1,))],
        compiler_params=pltpu.CompilerParams(
            collective_id=0, has_side_effects=True, vmem_limit_bytes=20 * 2**20
        ),
        name="halo",
    )(*[in_hbm(a) for a in (send_list, preact, cotangent, active)])
    windows = pl.pallas_call(
        window_kernel,
        out_shape=shaped((blocks, 9, (BS + 2) * BS * BS, LANES), jnp.bfloat16),
        in_specs=[smem, smem] + [vmem] * 4,
        out_specs=vmem,
        scratch_shapes=[pltpu.VMEM(((BS + 2) * CUBE_STEPS[0], LANES), jnp.float32)],
        compiler_params=pltpu.CompilerParams(vmem_limit_bytes=20 * 2**20),
        name="windows",
    )(in_hbm(owner_dir), in_hbm(owner_slot), split_grad, *landed)
    groups = stage_sizes(sizes)
    chunks = 1
    pair_tiles = channels // BS
    step = chunks * math.lcm(math.prod(groups), pair_tiles)
    tiles = -(-((taps + 1) // 2 * pair_tiles) // step) * step // chunks
    lengths = [tiles]
    for n in groups:
        lengths.append(lengths[-1] // n)
    result, full = pl.pallas_call(
        functools.partial(conv_kernel, sizes, chunks),
        out_shape=[
            shaped(features.shape, jnp.float32),
            shaped((chunks, tiles, BS, LANES), jnp.float32),
        ],
        in_specs=[vmem] * 5,
        out_specs=[vmem] * 2,
        scratch_shapes=[
            pltpu.VMEM((chunks, tiles, BS, LANES), jnp.float32),
            pltpu.VMEM((2 * channels, taps * LANES), jnp.bfloat16),
            pltpu.VMEM((2 * channels, blocks * volume), jnp.bfloat16),
        ]
        + [pltpu.VMEM((chunks, n, m, BS, LANES), jnp.float32) for n, m in zip(groups, lengths[1:])]
        + [pltpu.VMEM((chunks, m, BS, LANES), jnp.float32) for m in lengths[1:]]
        + [pltpu.SemaphoreType.DMA((chunks, n)) for n in groups for _ in range(4)],
        compiler_params=pltpu.CompilerParams(
            collective_id=1, has_side_effects=True, vmem_limit_bytes=32 * 2**20
        ),
        name="conv",
    )(windows, features, mask, kernel, bias)
    scaling = (volume * blocks * lax.axis_size(AXES)) ** (-0.5)
    input_grad, kernel_grad, bias_grad = pl.pallas_call(
        functools.partial(finish_kernel, scaling),
        out_shape=[
            shaped(features.shape, jnp.float32),
            shaped(kernel.shape, jnp.float32),
            shaped((1, channels), jnp.float32),
        ],
        in_specs=[vmem, pl.BlockSpec(memory_space=pl.ANY)],
        out_specs=[pl.BlockSpec(memory_space=pl.ANY), vmem, vmem],
        scratch_shapes=[pltpu.SemaphoreType.DMA((1,))],
        compiler_params=pltpu.CompilerParams(vmem_limit_bytes=16 * 2**20),
        name="finish",
    )(full, result)
    return input_grad, kernel_grad, bias_grad.reshape(channels)


def solution(mesh):
    whole = P(AXES, None, None)
    table = P(AXES, None)
    sizes = tuple(mesh.shape[axis] for axis in AXES)
    return jax.shard_map(
        functools.partial(shards, sizes),
        mesh=mesh,
        in_specs=(whole, whole, whole, P(), table, table, table, P(AXES)),
        out_specs=(whole, P(), P()),
        check_vma=False,
    )
```
